32 devices in a mesh: groups: 2 (over x), tm: 16 (over z, y, core).
Axes of the slice: x: 2, y: 2, z: 4, core: 2. Of those that a mesh axis runs over, the one named last changes fastest.
Arguments:
- signal: bfloat16 [128, 32768], P('groups', 'tm'), parts along dimension 0, may hold values from -24 to 24
- warp_blocks: int32 [4, 256], P('groups'), parts along dimension 0, may hold values from 0 to 255, as said below
- taps: int32 [4, 128, 8], P('groups'), parts along dimension 0, may hold values from 0 to 255
- tap_weights: float32 [4, 128, 8], P('groups'), parts along dimension 0, may hold values from -2 to 2
- replica: float32 [16384], replicated, may hold values from -0.046875 to 0.046875
Outputs:
- ambiguity: bfloat16 [4, 64, 32768], P('groups', None, 'tm'), parts along dimension 0
The draws below stay inside these ranges and needn't reach their ends.
There are 2 independent parts, one for each index of `groups`. The reference program is written for one: setup_inputs(seed, part) draws one part's arguments, and reference() takes and returns one part's arrays. A program takes and returns all parts, laid end to end along the dimension named above; an argument that names none is the same for every part. Nothing has to cross between parts.
Inputs may be any that keep to these rules, and one draw needn't show every extreme that they name: warp_blocks[h, j] = ((e_h + 128 * j + floor(r_h * 128 * j / 32768)) // 128) mod 256, with floor division, for an integer epoch e_h in 0 to 32767 and an integer rate r_h with -983 <= r_h <= 983, both drawn for each hypothesis; hypothesis 0 has e_0 = 32640. Consecutive entries of one hypothesis therefore differ by 0, 1 or 2 modulo 256.
All inputs are finite; a program needn't handle non-finite values.
Results may differ from the reference program's by a relative error of at most 0.0062.
Values may be sent and summed in bfloat16 or wider, within the bound.
No kernel may reach another device: no remote copies, remote signals or barrier semaphores. Data moves between devices by JAX's collectives and lax.ppermute only.
A program may use at most 64 MiB of HBM per device.

```python
import math
import jax
import jax.numpy as jnp
from jax import lax

BEAMS = 64
BLOCK = 128
TAPS = 8
FACTOR = 128
REPLICA = 16384
HYPS = 2
SAMPLES = 32768
NBLOCKS = 256


rate_limit = 983


knot_count = 8


def draw_signal(key, part):
    key = jax.random.fold_in(key, 5)
    value_key, beam_key, knot_key = jax.random.split(key, 3)
    loudness = jnp.exp(jax.random.uniform(beam_key, (BEAMS,), jnp.float32, 0.0, 1.0) * math.log(3.0))
    knots = jax.random.uniform(knot_key, (knot_count,), jnp.float32, 0.0, 1.0)
    times = jnp.arange(SAMPLES, dtype=jnp.int32) * knot_count
    lower = (times // SAMPLES).astype(jnp.int32)
    upper = ((lower + 1) % knot_count).astype(jnp.int32)
    fraction = (times % SAMPLES).astype(jnp.float32) / SAMPLES
    course = jnp.take(knots, lower) * (1.0 - fraction) + jnp.take(knots, upper) * fraction
    envelope = jnp.exp(course * math.log(3.0))
    values = jnp.clip(jax.random.normal(value_key, (BEAMS, SAMPLES), jnp.float32), -6.0, 6.0)
    values = values * loudness[:, None] * envelope[None, :]
    return jnp.clip(values, -24.0, 24.0).astype(jnp.bfloat16)


def draw_warp_blocks(key, part):
    key = jax.random.fold_in(key, 11)
    epoch_key, rate_key = jax.random.split(key)
    epochs = jax.random.randint(epoch_key, (HYPS,), 0, NBLOCKS * BLOCK, dtype=jnp.int32)
    epochs = jnp.where(jnp.arange(HYPS, dtype=jnp.int32) == 0, (NBLOCKS - 1) * BLOCK, epochs)
    rates = jax.random.randint(rate_key, (HYPS,), -rate_limit, rate_limit + 1, dtype=jnp.int32)
    starts = jnp.arange(NBLOCKS, dtype=jnp.int32) * BLOCK
    drift = rates[:, None] * starts[None, :] // 32768
    position = epochs[:, None] + starts[None, :] + drift
    return (position // BLOCK % NBLOCKS).astype(jnp.int32)


def place_ends(result, stream_key, least, high):
    dims = result.shape
    spot = [jax.random.randint(jax.random.fold_in(stream_key, axis), (), 0, dims[axis]) for axis in range(len(dims))]
    result = result.at[tuple(spot)].set(least)
    longest = dims.index(max(dims))
    spot[longest] = (spot[longest] + 1) % dims[longest]
    return result.at[tuple(spot)].set(high)


def noise(stream_key, dims, width, reach, held_as=jnp.bfloat16):
    array = width * jax.random.normal(stream_key, dims, jnp.float32)
    return jnp.clip(array, min=-reach, max=reach).astype(held_as)


def setup_inputs(seed: int = 0, part: int = 0) -> dict:
    streams_of = jax.random.split(jax.random.key(seed), 6)
    part_splits = jax.random.split(jax.random.fold_in(streams_of[5], part), 6)
    signal = draw_signal(jax.random.fold_in(jax.random.fold_in(streams_of[5], part), 71), part)
    warp_blocks = draw_warp_blocks(jax.random.fold_in(jax.random.fold_in(streams_of[5], part), 71), part)
    taps = place_ends(jax.random.randint(part_splits[2], (HYPS, BLOCK, TAPS), 0, 2 * BLOCK), jax.random.fold_in(part_splits[2], 1), 0, (2 * BLOCK) - 1).astype(jnp.int32)
    tap_weights = noise(part_splits[3], (HYPS, BLOCK, TAPS), TAPS ** -0.5, 2.0, jnp.float32)
    replica = noise(streams_of[4], (REPLICA,), (1.0 / FACTOR), 0.046875, jnp.float32)
    return dict(signal=signal, warp_blocks=warp_blocks, taps=taps, tap_weights=tap_weights, replica=replica)


def reference(signal, warp_blocks, taps, tap_weights, replica):
    samples = signal.shape[1]
    block_count = samples // BLOCK
    blocks = signal.reshape(BEAMS, block_count, BLOCK)
    padded = jnp.pad(replica, (0, samples - REPLICA))
    replica_spec = jnp.fft.rfft(padded)
    window_index = jnp.arange(2 * BLOCK, dtype=jnp.int32)
    results = []
    for hypothesis in range(HYPS):
        sources = warp_blocks[hypothesis].astype(jnp.int32)
        following = ((sources + 1) % block_count).astype(jnp.int32)
        windows = jnp.concatenate([blocks[:, sources], blocks[:, following]], axis=2)
        onehot = (taps[hypothesis][:, :, None] == window_index[None, None, :]).astype(jnp.float32)
        interp = jnp.einsum("ik,ikw->wi", tap_weights[hypothesis].astype(jnp.float32), onehot,
                            precision=lax.Precision.HIGHEST).astype(jnp.bfloat16)
        warped = jnp.dot(windows.reshape(-1, 2 * BLOCK), interp, preferred_element_type=jnp.float32)
        warped = lax.optimization_barrier(warped.astype(jnp.bfloat16)).astype(jnp.float32)
        warped = warped.reshape(BEAMS, samples)
        correlated = jnp.fft.irfft(jnp.fft.rfft(warped, axis=1) * jnp.conj(replica_spec)[None, :], n=samples, axis=1)
        power_map = correlated * correlated
        hyp_level = jnp.sum(power_map) / (BEAMS * samples) + 1e-6
        results.append((power_map / hyp_level).astype(jnp.bfloat16))
    return jnp.stack(results, 0)
```

```python
import functools

import jax
import jax.numpy as jnp
from jax import lax
from jax.experimental import pallas as pl
from jax.experimental.pallas import tpu as pltpu
from jax.sharding import PartitionSpec as P

BEAMS = 64
BLOCK = 128
PAIR = 2 * BLOCK
TAPS = 8
REPLICA = 16384
HYPS = 2
F32 = jnp.float32
BF16 = jnp.bfloat16

STRIPS = REPLICA // BLOCK + 2
STRIPS_PER_STEP = 10
TOEPLITZ_ROWS = STRIPS * BLOCK
NT = (((1,), (1,)), ((), ()))


def build_kernel(rev_ref, taps_ref, weights_ref, toeplitz_ref, interp_ref):
    step = pl.program_id(0)

    @pl.when(step == 0)
    def _():
        window = lax.broadcasted_iota(jnp.int32, (BLOCK, PAIR), 1)
        for hyp in range(HYPS):
            total = jnp.zeros((BLOCK, PAIR), F32)
            for tap in range(TAPS):
                hit = taps_ref[hyp, :, tap : tap + 1] == window
                total = total + jnp.where(hit, weights_ref[hyp, :, tap : tap + 1], 0.0)
            interp_ref[hyp * BLOCK : (hyp + 1) * BLOCK, :] = total.astype(BF16)

    previous = None
    for i in range(STRIPS_PER_STEP + 1):
        row = step * STRIPS_PER_STEP + i
        line = jnp.concatenate([rev_ref[pl.ds(row + 1, 1), :], rev_ref[pl.ds(row, 1), :]], axis=1)
        spread = jnp.broadcast_to(line, (BLOCK, PAIR))
        strip = pltpu.roll(spread, BLOCK, 1, stride=1, stride_axis=0)[:, :BLOCK].astype(BF16)
        if i > 0:
            rows = slice((i - 1) * BLOCK, i * BLOCK)
            toeplitz_ref[rows, :BLOCK] = strip
            toeplitz_ref[rows, BLOCK:] = previous
        previous = strip


def build(replica, taps, tap_weights):
    rev = jnp.pad(replica, (PAIR - 1, PAIR + 1)).reshape(-1, BLOCK)[:, ::-1]
    rows = STRIPS_PER_STEP * BLOCK
    return pl.pallas_call(
        build_kernel,
        grid=(STRIPS // STRIPS_PER_STEP,),
        out_shape=(
            jax.ShapeDtypeStruct((TOEPLITZ_ROWS, PAIR), BF16),
            jax.ShapeDtypeStruct((HYPS * BLOCK, PAIR), BF16),
        ),
        in_specs=[
            pl.BlockSpec(rev.shape, lambda g: (0, 0)),
            pl.BlockSpec(taps.shape, lambda g: (0, 0, 0)),
            pl.BlockSpec(tap_weights.shape, lambda g: (0, 0, 0)),
        ],
        out_specs=(
            pl.BlockSpec((rows, PAIR), lambda g: (g, 0)),
            pl.BlockSpec((HYPS * BLOCK, PAIR), lambda g: (0, 0)),
        ),
        cost_estimate=pl.CostEstimate(flops=10_000_000, bytes_accessed=16_000_000, transcendentals=0),
        name="build_toeplitz",
    )(rev, taps, tap_weights)


def split_sum(total):
    high = total.astype(BF16).astype(F32)
    middle = (total - high).astype(BF16).astype(F32)
    return high, middle, total - high - middle


def correlate_kernel(plan, sources_ref, source_ref, interp_ref, toeplitz_hbm, out_ref, wide_ref, acc_ref, toeplitz_ref, sems, *scratch):
    lines, wide, steps, segments = plan["lines"], plan["wide"], plan["steps"], plan["segments"]
    rows = acc_ref.shape[0]
    depth = wide * PAIR
    blocks = rows // lines

    def fetch(step):
        start = step * depth
        size = min(depth, TOEPLITZ_ROWS - start)
        part = pl.ds(start, size)
        return pltpu.make_async_copy(toeplitz_hbm.at[part, :], toeplitz_ref.at[part, :], sems.at[step])

    for step in range(steps):
        fetch(step).start()

    if plan["fused"]:
        next_ref, first_ref, second_ref, warped_ref = scratch
        beams = lines // HYPS
        chunk = 256

        def product(start, half):
            return lax.dot_general(
                source_ref[pl.ds(start, chunk), :],
                interp_ref[:, half * BLOCK : (half + 1) * BLOCK],
                NT,
                preferred_element_type=F32,
            )

        for start in range(0, rows, chunk):
            next_ref[start : start + chunk, :] = product(start, 1)
        next_ref[rows : rows + 8, :] = next_ref[0:8, :]
        for start in range(0, rows, chunk):
            value = product(start, 0) + next_ref[start + beams : start + beams + chunk, :]
            first_ref[start : start + chunk, :] = value[:, :BLOCK]
            second_ref[start + beams : start + beams + chunk, :] = value[:, BLOCK:]
        upper = lax.broadcasted_iota(jnp.int32, (lines, BLOCK), 0) < beams

        unroll = 8

        def gather(group, carry):
            for inner in range(unroll):
                block = group * unroll + inner
                for half in range(2):
                    at_first = sources_ref[0, 2 * block + half] * beams
                    at_second = sources_ref[1, 2 * block + half] * beams
                    value = jnp.where(
                        upper, first_ref[pl.ds(at_first, lines), :], second_ref[pl.ds(at_second, lines), :]
                    )
                    warped_ref[pl.ds(pl.multiple_of(block * lines, lines), lines), half * BLOCK : (half + 1) * BLOCK] = value
            return carry

        lax.fori_loop(0, blocks // unroll, gather, 0)
        extra = warped_ref.shape[0] - rows
        warped_ref[rows:, :] = warped_ref[:extra, :]
        piece = 256
        for start in range(0, wide_ref.shape[0], piece):
            for shift in range(wide):
                from_row = start + shift * lines
                wide_ref[start : start + piece, shift * PAIR : (shift + 1) * PAIR] = warped_ref[
                    from_row : from_row + piece, :
                ].astype(BF16)
    else:
        wide_ref[...] = source_ref[...]

    def step_product(step, offset):
        return jnp.dot(
            wide_ref[pl.ds(offset, rows), :],
            toeplitz_ref[pl.ds(step * depth, depth), :],
            preferred_element_type=F32,
        )

    fetch(0).wait()
    acc_ref[...] = step_product(0, 0)

    whole = TOEPLITZ_ROWS // depth
    for step in range(1, whole):
        fetch(step).wait()
        acc_ref[...] += step_product(step, step * wide * lines)
    if whole < steps:
        fetch(whole).wait()
        left = TOEPLITZ_ROWS - whole * depth
        acc_ref[...] += jnp.dot(
            wide_ref[whole * wide * lines : whole * wide * lines + rows, :left],
            toeplitz_ref[whole * depth :, :],
            preferred_element_type=F32,
        )

    share = rows // segments
    sums = jnp.zeros((8, PAIR), F32)
    for segment in range(segments):
        value = acc_ref[segment * share : (segment + 1) * share, :]
        power = value * value
        sums = sums + jnp.sum(power.reshape(share // 8, 8, PAIR), axis=0)
        out_ref[segment, :share, :] = power[:, :BLOCK].astype(BF16)
        out_ref[segment, share : 2 * share, :] = power[:, BLOCK:].astype(BF16)
    sums = jnp.sum(sums, axis=1, keepdims=True)
    line = lax.broadcasted_iota(jnp.int32, (8, 1), 0)
    is_first = line % lines < lines // HYPS
    place = lax.broadcasted_iota(jnp.int32, (16, BLOCK), 0)
    tail = jnp.zeros((16, BLOCK), F32)
    for hyp in range(HYPS):
        total = jnp.sum(jnp.where(is_first == (hyp == 0), sums, 0.0), axis=0, keepdims=True)
        for index, part in enumerate(split_sum(total)):
            tail = jnp.where(place == hyp * 3 + index, part, tail)
    tail = tail.astype(BF16)
    for segment in range(segments):
        out_ref[segment, 2 * share :, :] = tail


def correlate(plan, sources, source, interp, toeplitz):
    lines, wide, steps, segments, rows = (plan[k] for k in ("lines", "wide", "steps", "segments", "rows"))
    wide_rows = rows + REPLICA // PAIR * lines
    share = rows // segments
    scratch = [
        pltpu.VMEM((wide_rows, wide * PAIR), BF16),
        pltpu.VMEM((rows, PAIR), F32),
        pltpu.VMEM((TOEPLITZ_ROWS, PAIR), BF16),
        pltpu.SemaphoreType.DMA((steps,)),
    ]
    if plan["fused"]:
        scratch += [
            pltpu.VMEM((rows + 8, PAIR), F32),
            pltpu.VMEM((rows + 8, BLOCK), F32),
            pltpu.VMEM((rows + 8, BLOCK), F32),
            pltpu.VMEM((wide_rows + wide * lines, PAIR), F32),
        ]
    vmem = pl.BlockSpec(memory_space=pltpu.VMEM)
    return pl.pallas_call(
        functools.partial(correlate_kernel, plan),
        out_shape=jax.ShapeDtypeStruct((segments, 2 * share + 16, BLOCK), BF16),
        in_specs=[pl.BlockSpec(memory_space=pltpu.SMEM), vmem, vmem, pl.BlockSpec(memory_space=pl.ANY)],
        out_specs=vmem,
        scratch_shapes=scratch,
        compiler_params=pltpu.CompilerParams(vmem_limit_bytes=48 * 1024 * 1024),
        cost_estimate=pl.CostEstimate(
            flops=2 * rows * TOEPLITZ_ROWS * PAIR, bytes_accessed=12_000_000, transcendentals=0
        ),
        name="warp_correlate",
    )(sources, source, interp, toeplitz)


def levels_of(sums, count):
    return [jnp.sum(sums[:, 3 * hyp : 3 * hyp + 3, :1]) / count + 1e-06 for hyp in range(HYPS)]


def finish_kernel(count, power_ref, sums_ref, out_ref):
    sums = sums_ref[...].astype(F32)
    upper = lax.broadcasted_iota(jnp.int32, (8, BLOCK), 0) < 4
    place = lax.broadcasted_iota(jnp.int32, sums.shape, 1)
    inverse = []
    for hyp in range(HYPS):
        picked = jnp.where((place >= 3 * hyp) & (place < 3 * hyp + 3), sums, 0.0)
        total = jnp.sum(jnp.sum(picked, axis=0), axis=0, keepdims=True)
        inverse.append(1.0 / (total / count + 1e-06))
    scale = jnp.where(upper, inverse[0], inverse[1])
    for half in range(2):
        for pair in range(4):
            tiles = [
                power_ref[device, half * 64 + pair * 16 : half * 64 + pair * 16 + 16, :].astype(F32)
                for device in range(4)
            ]
            for inner in range(2):
                parts = [tile[inner * 8 : inner * 8 + 8, :] * scale for tile in tiles]
                turned = [pltpu.roll(part, 4, 0) for part in parts]
                lane = (pair * 2 + inner) * PAIR + half * BLOCK
                low = [jnp.where(upper, parts[d], turned[d + 1]) for d in (0, 2)]
                high = [jnp.where(upper, turned[d], parts[d + 1]) for d in (0, 2)]
                out_ref[0, :, lane : lane + BLOCK] = jnp.concatenate(low, axis=0).astype(BF16)
                out_ref[1, :, lane : lane + BLOCK] = jnp.concatenate(high, axis=0).astype(BF16)


def finish(received, count):
    segments = received.shape[0]
    return pl.pallas_call(
        functools.partial(finish_kernel, count),
        grid=(segments // 4,),
        out_shape=jax.ShapeDtypeStruct((HYPS, segments * 4, 8 * PAIR), BF16),
        in_specs=[
            pl.BlockSpec((4, 144, BLOCK), lambda g: (g, 0, 0)),
            pl.BlockSpec((segments, 16, BLOCK), lambda g: (0, 8, 0)),
        ],
        out_specs=pl.BlockSpec((HYPS, 16, 8 * PAIR), lambda g: (0, g, 0)),
        cost_estimate=pl.CostEstimate(flops=1_000_000, bytes_accessed=1_200_000, transcendentals=0),
        name="scale_power",
    )(received, received)


def finish_plain(received, count, lines):
    segments = received.shape[0]
    beams = lines // HYPS
    blocks = (received.shape[1] - 16) // (2 * lines)
    levels = jnp.stack(levels_of(received[:, -16:, :].astype(F32), count))
    power = received[:, :-16, :].reshape(segments, 2, blocks, HYPS, beams, BLOCK).astype(F32)
    scaled = (power / levels[:, None, None]).astype(BF16)
    return scaled.transpose(3, 0, 4, 2, 1, 5).reshape(HYPS, segments * beams, blocks * PAIR)


def widen(received, sources, interp, beams, wide, wide_blocks):
    blocks = received.reshape(-1, beams, BLOCK)
    windows = jnp.concatenate([blocks, jnp.roll(blocks, -1, axis=0)], axis=2)
    warped = lax.dot_general(
        windows, interp, (((2,), (1,)), ((), ())), preferred_element_type=F32
    ).astype(BF16)
    warped = warped.reshape(-1, beams, HYPS, BLOCK)
    chosen = jnp.stack([jnp.take(warped[:, :, hyp], sources[hyp], axis=0) for hyp in range(HYPS)], axis=1)
    count = chosen.shape[0] // 2
    pairs = chosen.reshape(count, 2, HYPS, beams, BLOCK).transpose(0, 2, 3, 1, 4)
    pairs = pairs.reshape(count, HYPS * beams, PAIR)
    index = jnp.arange(wide_blocks)
    spread = [jnp.take(pairs, (index + shift) % count, axis=0) for shift in range(wide)]
    return jnp.concatenate(spread, axis=2).reshape(wide_blocks * HYPS * beams, wide * PAIR)


def body(signal, warp_blocks, taps, tap_weights, replica):
    segments = lax.axis_size("tm")
    beams = signal.shape[0] // segments
    samples = signal.shape[1] * segments
    local = signal.shape[1] // BLOCK
    lines = HYPS * beams
    send = signal.reshape(segments, beams, local, BLOCK).transpose(0, 2, 1, 3)
    send = send.reshape(segments, local * beams, BLOCK)
    received = lax.all_to_all(send, "tm", split_axis=0, concat_axis=0, tiled=True)
    toeplitz, interp = build(replica, taps, tap_weights)
    wide = max(2, 16 // lines)
    plan = dict(
        lines=lines,
        wide=wide,
        steps=-(-TOEPLITZ_ROWS // (wide * PAIR)),
        segments=segments,
        rows=samples // PAIR * lines,
        fused=lines == 8,
    )
    if plan["fused"]:
        source = received.reshape(-1, BLOCK)
    else:
        source = widen(received, warp_blocks, interp, beams, wide, samples // PAIR + REPLICA // PAIR)
    sent = correlate(plan, warp_blocks, source, interp, toeplitz)
    back = lax.all_to_all(sent, "tm", split_axis=0, concat_axis=0, tiled=True)
    count = float(BEAMS * samples)
    if plan["fused"] and signal.shape[1] == 8 * PAIR:
        return finish(back, count)
    return finish_plain(back, count, lines)


def solution(mesh):
    in_specs = (
        P("groups", "tm"),
        P("groups", None),
        P("groups", None, None),
        P("groups", None, None),
        P(),
    )
    out_specs = P("groups", None, "tm")
    return jax.shard_map(body, mesh=mesh, in_specs=in_specs, out_specs=out_specs, check_vma=False)
```

```python
import functools

import jax
import jax.numpy as jnp
from jax import lax
from jax.experimental import pallas as pl
from jax.experimental.pallas import tpu as pltpu
from jax.sharding import PartitionSpec as P

BEAMS = 64
BLOCK = 128
PAIR = 2 * BLOCK
TAPS = 8
REPLICA = 16384
HYPS = 2
F32 = jnp.float32
BF16 = jnp.bfloat16

STRIPS = REPLICA // BLOCK + 2
STRIPS_PER_LOOP = 10
TOEPLITZ_ROWS = STRIPS * BLOCK
VMEM = pl.BlockSpec(memory_space=pltpu.VMEM)


def spread_kernel(signal_ref, out_ref):
    upper = lax.broadcasted_iota(jnp.int32, (8, BLOCK), 0) < 4
    groups, blocks = signal_ref.shape[0] // 16, signal_ref.shape[1] // BLOCK
    for group in range(groups):
        for quad in range(0, blocks, 4):
            tiles = []
            for block in range(quad, quad + 4):
                value = signal_ref[group * 16 : group * 16 + 16, block * BLOCK : (block + 1) * BLOCK].astype(F32)
                tiles.append((value[:8], value[8:]))
            for half in range(2):
                parts = [tile[half] for tile in tiles]
                turned = [pltpu.roll(part, 4, 0) for part in parts]
                first = [jnp.where(upper, parts[d], turned[d + 1]) for d in (0, 2)]
                second = [jnp.where(upper, turned[d], parts[d + 1]) for d in (0, 2)]
                device = group * 4 + half * 2
                rows = slice(quad * 4, quad * 4 + 16)
                out_ref[device, rows, :] = jnp.concatenate(first, axis=0).astype(BF16)
                out_ref[device + 1, rows, :] = jnp.concatenate(second, axis=0).astype(BF16)


def spread(signal, segments):
    beams, blocks = signal.shape[0] // segments, signal.shape[1] // BLOCK
    if beams != 4 or signal.shape[0] % 16 or blocks % 4:
        send = signal.reshape(segments, beams, blocks, BLOCK).transpose(0, 2, 1, 3)
        return send.reshape(segments, blocks * beams, BLOCK)
    return pl.pallas_call(
        spread_kernel,
        out_shape=jax.ShapeDtypeStruct((segments, blocks * beams, BLOCK), BF16),
        in_specs=[VMEM],
        out_specs=VMEM,
        name="spread_beams",
    )(signal)


def build_kernel(replica_ref, taps_ref, weights_ref, strips_ref, interp_ref, line_ref):
    window = lax.broadcasted_iota(jnp.int32, (PAIR, BLOCK), 0)
    for hyp in range(HYPS):
        total = jnp.zeros((PAIR, BLOCK), F32)
        for tap in range(TAPS):
            hit = taps_ref[hyp, tap : tap + 1, :] == window
            total = total + jnp.where(hit, weights_ref[hyp, tap : tap + 1, :], 0.0)
        interp_ref[:, hyp * BLOCK : (hyp + 1) * BLOCK] = total.astype(BF16)

    count = replica_ref.shape[0]
    row = lax.broadcasted_iota(jnp.int32, (BLOCK, BLOCK), 0)
    col = lax.broadcasted_iota(jnp.int32, (BLOCK, BLOCK), 1)
    keep = ((row == 0) & (col == 0)).astype(F32).astype(BF16)
    turn = ((row + col == BLOCK) & (col > 0)).astype(F32).astype(BF16)
    rounded = replica_ref[...].astype(BF16)
    line_ref[...] = jnp.zeros_like(line_ref)
    line_ref[1 : count + 1, :] = jnp.dot(rounded, keep, preferred_element_type=F32)
    line_ref[2 : count + 2, :] += jnp.dot(rounded, turn, preferred_element_type=F32)
    below = col >= row

    def rotations(index):
        line = jnp.broadcast_to(line_ref[pl.ds(index, 1), :], (BLOCK, BLOCK))
        return pltpu.roll(line, 0, 1, stride=1, stride_axis=0)

    def some(group, now):
        for inner in range(STRIPS_PER_LOOP):
            strip = group * STRIPS_PER_LOOP + inner
            after = rotations(strip + 1)
            rows = pl.ds(pl.multiple_of(strip * BLOCK, BLOCK), BLOCK)
            strips_ref[rows, :] = jnp.where(below, now, after).astype(BF16)
            now = after
        return now

    lax.fori_loop(0, STRIPS // STRIPS_PER_LOOP, some, rotations(0))
    strips_ref[STRIPS * BLOCK :, :] = jnp.zeros((BLOCK, BLOCK), BF16)


def build(replica, taps, tap_weights):
    return pl.pallas_call(
        build_kernel,
        out_shape=(
            jax.ShapeDtypeStruct((TOEPLITZ_ROWS + BLOCK, BLOCK), BF16),
            jax.ShapeDtypeStruct((PAIR, HYPS * BLOCK), BF16),
        ),
        in_specs=[VMEM] * 3,
        out_specs=(VMEM, VMEM),
        scratch_shapes=[pltpu.VMEM((STRIPS + 14, BLOCK), F32)],
        compiler_params=pltpu.CompilerParams(vmem_limit_bytes=16 * 1024 * 1024),
        cost_estimate=pl.CostEstimate(flops=10_000_000, bytes_accessed=16_000_000, transcendentals=0),
        name="build_toeplitz",
    )(replica.reshape(-1, BLOCK), taps.transpose(0, 2, 1), tap_weights.transpose(0, 2, 1))


def split_sum(total):
    high = total.astype(BF16).astype(F32)
    middle = (total - high).astype(BF16).astype(F32)
    return high, middle, total - high - middle


def warp_rows(sources_ref, source_ref, interp_ref, wide_ref, next_ref, warped_ref):
    rows = source_ref.shape[0]
    blocks = rows // 8
    upper = lax.broadcasted_iota(jnp.int32, (8, BLOCK), 0) < 4
    chunk = 256

    def product(start, half):
        return jnp.dot(
            source_ref[start : start + chunk, :],
            interp_ref[half * BLOCK : (half + 1) * BLOCK, :],
            preferred_element_type=F32,
        )

    for start in range(0, rows, chunk):
        next_ref[start : start + chunk, :] = product(start, 1)
    next_ref[rows : rows + 8, :] = next_ref[0:8, :]
    for start in range(0, rows, chunk):
        value = product(start, 0) + next_ref[start + 4 : start + 4 + chunk, :]
        first = value[:, :BLOCK].reshape(chunk // 8, 8, BLOCK)
        second = value[:, BLOCK:].reshape(chunk // 8, 8, BLOCK)
        even = jnp.where(upper, first, pltpu.roll(second, 4, 1))
        odd = jnp.where(upper, pltpu.roll(first, 4, 1), second)
        both = jnp.stack([even, odd], axis=1).reshape(2 * chunk, BLOCK)
        warped_ref[2 * start : 2 * start + 2 * chunk, :] = both

    def block_of(index):
        halves = []
        for half in range(2):
            picked = [
                warped_ref[pl.ds(pl.multiple_of(sources_ref[hyp, 2 * index + half] * 8, 8), 8), :]
                for hyp in range(HYPS)
            ]
            halves.append(jnp.where(upper, picked[0], picked[1]))
        return jnp.concatenate(halves, axis=1)

    unroll = 4

    def gather(group, before):
        for inner in range(unroll):
            pair = group * unroll + inner
            now, after = block_of(2 * pair), block_of(2 * pair + 1)
            place = pl.multiple_of(pair * 16, 16)
            wide_ref[pl.ds(place + 16, 16), :PAIR] = jnp.concatenate([now, after], axis=0).astype(BF16)
            wide_ref[pl.ds(place, 16), PAIR:] = jnp.concatenate([before, now], axis=0).astype(BF16)
            before = after
        return before

    last = lax.fori_loop(0, blocks // 2 // unroll, gather, jnp.zeros((8, PAIR), F32))
    wide_ref[rows : rows + 16, PAIR:] = jnp.concatenate([last, block_of(0)], axis=0).astype(BF16)
    extra = wide_ref.shape[0] - 16 - rows
    wide_ref[16 + rows :, :] = wide_ref[16 : 16 + extra, :]


def correlate_kernel(plan, sources_ref, source_ref, interp_ref, strips_ref, out_ref, wide_ref, acc_ref, *scratch):
    lines, wide, segments = plan["lines"], plan["wide"], plan["segments"]
    rows = acc_ref.shape[0]
    depth = wide * PAIR
    if plan["fused"]:
        warp_rows(sources_ref, source_ref, interp_ref, wide_ref, *scratch)
        base = 16
    else:
        wide_ref[...] = source_ref[...]
        base = 0

    parts = 2
    part = rows // parts
    share = rows // segments
    sums = jnp.zeros((8, PAIR), F32)
    for index in range(parts):
        for start in range(0, TOEPLITZ_ROWS, depth):
            size = min(depth, TOEPLITZ_ROWS - start)
            matrix = jnp.concatenate(
                [strips_ref[start + BLOCK : start + BLOCK + size, :], strips_ref[start : start + size, :]], axis=1
            )
            offset = base + index * part + start // PAIR * lines
            value = jnp.dot(wide_ref[offset : offset + part, :size], matrix, preferred_element_type=F32)
            if start == 0:
                acc_ref[index * part : (index + 1) * part, :] = value
            else:
                acc_ref[index * part : (index + 1) * part, :] += value
        for segment in range(index * segments // parts, (index + 1) * segments // parts):
            value = acc_ref[segment * share : (segment + 1) * share, :]
            power = value * value
            sums = sums + jnp.sum(power.reshape(share // 8, 8, PAIR), axis=0)
            out_ref[segment, :share, :] = power[:, :BLOCK].astype(BF16)
            out_ref[segment, share : 2 * share, :] = power[:, BLOCK:].astype(BF16)
    sums = jnp.sum(sums, axis=1, keepdims=True)
    line = lax.broadcasted_iota(jnp.int32, (8, 1), 0)
    is_first = line % lines < lines // HYPS
    place = lax.broadcasted_iota(jnp.int32, (16, BLOCK), 0)
    tail = jnp.zeros((16, BLOCK), F32)
    for hyp in range(HYPS):
        total = jnp.sum(jnp.where(is_first == (hyp == 0), sums, 0.0), axis=0, keepdims=True)
        for index, piece in enumerate(split_sum(total)):
            tail = jnp.where(place == hyp * 3 + index, piece, tail)
    tail = tail.astype(BF16)
    for segment in range(segments):
        out_ref[segment, 2 * share :, :] = tail


def correlate(plan, sources, source, interp, strips):
    lines, wide, segments, rows = (plan[k] for k in ("lines", "wide", "segments", "rows"))
    wide_rows = rows + REPLICA // PAIR * lines
    share = rows // segments
    scratch = [pltpu.VMEM((wide_rows + (16 if plan["fused"] else 0), wide * PAIR), BF16), pltpu.VMEM((rows, PAIR), F32)]
    if plan["fused"]:
        scratch += [pltpu.VMEM((rows + 8, PAIR), F32), pltpu.VMEM((2 * rows, BLOCK), F32)]
    return pl.pallas_call(
        functools.partial(correlate_kernel, plan),
        out_shape=jax.ShapeDtypeStruct((segments, 2 * share + 16, BLOCK), BF16),
        in_specs=[pl.BlockSpec(memory_space=pltpu.SMEM), VMEM, VMEM, VMEM],
        out_specs=VMEM,
        scratch_shapes=scratch,
        compiler_params=pltpu.CompilerParams(vmem_limit_bytes=24 * 1024 * 1024),
        cost_estimate=pl.CostEstimate(
            flops=2 * rows * TOEPLITZ_ROWS * PAIR, bytes_accessed=12_000_000, transcendentals=0
        ),
        name="warp_correlate",
    )(sources, source, interp, strips)


def levels_of(sums, count):
    return [jnp.sum(sums[:, 3 * hyp : 3 * hyp + 3, :1]) / count + 1e-06 for hyp in range(HYPS)]


def finish_kernel(count, power_ref, sums_ref, out_ref):
    sums = sums_ref[...].astype(F32)
    upper = lax.broadcasted_iota(jnp.int32, (8, BLOCK), 0) < 4
    place = lax.broadcasted_iota(jnp.int32, sums.shape, 1)
    inverse = []
    for hyp in range(HYPS):
        picked = jnp.where((place >= 3 * hyp) & (place < 3 * hyp + 3), sums, 0.0)
        total = jnp.sum(jnp.sum(picked, axis=0), axis=0, keepdims=True)
        inverse.append(1.0 / (total / count + 1e-06))
    scale = jnp.where(upper, inverse[0], inverse[1])
    for half in range(2):
        for pair in range(4):
            tiles = [
                power_ref[device, half * 64 + pair * 16 : half * 64 + pair * 16 + 16, :].astype(F32)
                for device in range(4)
            ]
            for inner in range(2):
                parts = [tile[inner * 8 : inner * 8 + 8, :] * scale for tile in tiles]
                turned = [pltpu.roll(part, 4, 0) for part in parts]
                lane = (pair * 2 + inner) * PAIR + half * BLOCK
                low = [jnp.where(upper, parts[d], turned[d + 1]) for d in (0, 2)]
                high = [jnp.where(upper, turned[d], parts[d + 1]) for d in (0, 2)]
                out_ref[0, :, lane : lane + BLOCK] = jnp.concatenate(low, axis=0).astype(BF16)
                out_ref[1, :, lane : lane + BLOCK] = jnp.concatenate(high, axis=0).astype(BF16)


def finish(received, count):
    segments = received.shape[0]
    return pl.pallas_call(
        functools.partial(finish_kernel, count),
        grid=(segments // 4,),
        out_shape=jax.ShapeDtypeStruct((HYPS, segments * 4, 8 * PAIR), BF16),
        in_specs=[
            pl.BlockSpec((4, 144, BLOCK), lambda g: (g, 0, 0)),
            pl.BlockSpec((segments, 16, BLOCK), lambda g: (0, 8, 0)),
        ],
        out_specs=pl.BlockSpec((HYPS, 16, 8 * PAIR), lambda g: (0, g, 0)),
        cost_estimate=pl.CostEstimate(flops=1_000_000, bytes_accessed=1_200_000, transcendentals=0),
        name="scale_power",
    )(received, received)


def finish_plain(received, count, lines):
    segments = received.shape[0]
    beams = lines // HYPS
    blocks = (received.shape[1] - 16) // (2 * lines)
    levels = jnp.stack(levels_of(received[:, -16:, :].astype(F32), count))
    power = received[:, :-16, :].reshape(segments, 2, blocks, HYPS, beams, BLOCK).astype(F32)
    scaled = (power / levels[:, None, None]).astype(BF16)
    return scaled.transpose(3, 0, 4, 2, 1, 5).reshape(HYPS, segments * beams, blocks * PAIR)


def widen(received, sources, interp, beams, wide, wide_blocks):
    blocks = received.reshape(-1, beams, BLOCK)
    windows = jnp.concatenate([blocks, jnp.roll(blocks, -1, axis=0)], axis=2)
    warped = lax.dot_general(
        windows, interp, (((2,), (0,)), ((), ())), preferred_element_type=F32
    ).astype(BF16)
    warped = warped.reshape(-1, beams, HYPS, BLOCK)
    chosen = jnp.stack([jnp.take(warped[:, :, hyp], sources[hyp], axis=0) for hyp in range(HYPS)], axis=1)
    count = chosen.shape[0] // 2
    pairs = chosen.reshape(count, 2, HYPS, beams, BLOCK).transpose(0, 2, 3, 1, 4)
    pairs = pairs.reshape(count, HYPS * beams, PAIR)
    index = jnp.arange(wide_blocks)
    spread = [jnp.take(pairs, (index + shift) % count, axis=0) for shift in range(wide)]
    return jnp.concatenate(spread, axis=2).reshape(wide_blocks * HYPS * beams, wide * PAIR)


def body(signal, warp_blocks, taps, tap_weights, replica):
    segments = lax.axis_size("tm")
    beams = signal.shape[0] // segments
    samples = signal.shape[1] * segments
    lines = HYPS * beams
    received = lax.all_to_all(spread(signal, segments), "tm", split_axis=0, concat_axis=0, tiled=True)
    strips, interp = build(replica, taps, tap_weights)
    wide = max(2, 16 // lines)
    plan = dict(
        lines=lines,
        wide=wide,
        segments=segments,
        rows=samples // PAIR * lines,
        fused=lines == 8,
    )
    if plan["fused"]:
        source = received.reshape(-1, BLOCK)
    else:
        source = widen(received, warp_blocks, interp, beams, wide, samples // PAIR + REPLICA // PAIR)
    sent = correlate(plan, warp_blocks, source, interp, strips)
    back = lax.all_to_all(sent, "tm", split_axis=0, concat_axis=0, tiled=True)
    count = float(BEAMS * samples)
    if plan["fused"] and signal.shape[1] == 8 * PAIR:
        return finish(back, count)
    return finish_plain(back, count, lines)


def solution(mesh):
    in_specs = (
        P("groups", "tm"),
        P("groups", None),
        P("groups", None, None),
        P("groups", None, None),
        P(),
    )
    out_specs = P("groups", None, "tm")
    return jax.shard_map(body, mesh=mesh, in_specs=in_specs, out_specs=out_specs, check_vma=False)
```

```python
import functools
import math

import jax
import jax.numpy as jnp
import numpy as np
from jax import lax
from jax.experimental import pallas as pl
from jax.experimental.pallas import tpu as pltpu
from jax.sharding import PartitionSpec as P

BEAMS = 64
BLOCK = 128
PAIR = 2 * BLOCK
TAPS = 8
REPLICA = 16384
HYPS = 2
F32 = jnp.float32
BF16 = jnp.bfloat16
VMEM = pl.BlockSpec(memory_space=pltpu.VMEM)
ANY = pl.BlockSpec(memory_space=pl.ANY)


def transform_tables(points):
    k, p = np.arange(points)[:, None], np.arange(points)[None, :]
    angle = 2.0 * math.pi * (k * p % points) / points
    cos, sin = np.cos(angle), np.sin(angle)
    left = np.block([[cos, sin], [-sin, cos]]).astype(np.float32)
    k, p = np.arange(PAIR)[:, None], np.arange(PAIR)[None, :]
    angle = 2.0 * math.pi * (k * p % PAIR) / PAIR
    cos, sin = np.cos(angle), np.sin(angle)
    right = np.block([[cos, -sin], [sin, cos]]).astype(np.float32)
    k, q = np.arange(points)[:, None], np.arange(PAIR)[None, :]
    angle = 2.0 * math.pi * (k * q) / (points * PAIR)
    turn = np.concatenate([np.cos(angle), -np.sin(angle)], axis=1).astype(np.float32)
    parts = []
    for table in (left, right):
        high = table.astype(jnp.bfloat16)
        low = (table - high.astype(np.float32)).astype(jnp.bfloat16)
        parts.append(np.concatenate([high, low], axis=0))
    return jnp.asarray(parts[0]), jnp.asarray(parts[1]), jnp.asarray(turn)


def split(value):
    high = value.astype(BF16)
    return high, (value - high.astype(F32)).astype(BF16)


def dot(left, right):
    return jnp.dot(left, right, preferred_element_type=F32)


def spread_kernel(signal_ref, out_ref):
    upper = lax.broadcasted_iota(jnp.int32, (8, BLOCK), 0) < 4
    groups, blocks = signal_ref.shape[0] // 16, signal_ref.shape[1] // BLOCK
    for group in range(groups):
        for quad in range(0, blocks, 4):
            tiles = []
            for block in range(quad, quad + 4):
                value = signal_ref[group * 16 : group * 16 + 16, block * BLOCK : (block + 1) * BLOCK].astype(F32)
                tiles.append((value[:8], value[8:]))
            for half in range(2):
                parts = [tile[half] for tile in tiles]
                turned = [pltpu.roll(part, 4, 0) for part in parts]
                first = [jnp.where(upper, parts[d], turned[d + 1]) for d in (0, 2)]
                second = [jnp.where(upper, turned[d], parts[d + 1]) for d in (0, 2)]
                device = group * 4 + half * 2
                rows = slice(quad * 4, quad * 4 + 16)
                out_ref[device, rows, :] = jnp.concatenate(first, axis=0).astype(BF16)
                out_ref[device + 1, rows, :] = jnp.concatenate(second, axis=0).astype(BF16)


def spread(signal, segments):
    beams, blocks = signal.shape[0] // segments, signal.shape[1] // BLOCK
    if beams != 4 or signal.shape[0] % 16 or blocks % 4:
        send = signal.reshape(segments, beams, blocks, BLOCK).transpose(0, 2, 1, 3)
        return send.reshape(segments, blocks * beams, BLOCK)
    return pl.pallas_call(
        spread_kernel,
        out_shape=jax.ShapeDtypeStruct((segments, blocks * beams, BLOCK), BF16),
        in_specs=[VMEM],
        out_specs=VMEM,
        name="spread_beams",
    )(signal)


def prepare_kernel(replica_ref, taps_ref, weights_ref, sources_ref, left_ref, right_ref, turn_ref, interp_ref, chosen_ref, spectrum_ref):
    window = lax.broadcasted_iota(jnp.int32, (PAIR, BLOCK), 0)
    for hyp in range(HYPS):
        total = jnp.zeros((PAIR, BLOCK), F32)
        for tap in range(TAPS):
            hit = taps_ref[hyp, tap : tap + 1, :] == window
            total = total + jnp.where(hit, weights_ref[hyp, tap : tap + 1, :], 0.0)
        interp_ref[:, hyp * BLOCK : (hyp + 1) * BLOCK] = total.astype(BF16)

    blocks = chosen_ref.shape[1]
    column = lax.broadcasted_iota(jnp.int32, (blocks, blocks), 1)
    for hyp in range(HYPS):
        rows = slice(hyp * blocks, (hyp + 1) * blocks)
        chosen_ref[rows, :] = (sources_ref[rows, :] == column).astype(F32).astype(BF16)

    points = turn_ref.shape[0]
    lines = replica_ref.shape[0]
    high, low = split(replica_ref[...])
    both = dot(left_ref[:, :lines], high)
    value = both[: 2 * points] + both[2 * points :] + dot(left_ref[: 2 * points, :lines], low)
    value_re, value_im = value[:points], value[points:]
    turn_re, turn_im = turn_ref[:, :PAIR], turn_ref[:, PAIR:]
    turned = jnp.concatenate(
        [value_re * turn_re - value_im * turn_im, value_re * turn_im + value_im * turn_re], axis=1
    )
    high, low = split(turned)
    upper, lower = right_ref[: 2 * PAIR, :], right_ref[2 * PAIR :, :]
    value = (dot(high, upper) + dot(high, lower) + dot(low, upper)) * (1.0 / (points * PAIR))
    spectrum_ref[:, :PAIR] = value[:, :PAIR]
    spectrum_ref[:, PAIR:] = -value[:, PAIR:]


def prepare(replica, taps, tap_weights, warp_blocks, tables):
    blocks = warp_blocks.shape[1]
    points = blocks // 2
    ordered = warp_blocks.reshape(HYPS, points, 2).transpose(0, 2, 1).reshape(HYPS * blocks, 1)
    operands = (replica.reshape(-1, PAIR), taps.transpose(0, 2, 1), tap_weights.transpose(0, 2, 1), ordered, *tables)
    shapes = ((PAIR, HYPS * BLOCK), BF16), ((HYPS * blocks, blocks), BF16), ((points, 2 * PAIR), F32)

    def whole(shape):
        return pl.BlockSpec(shape, lambda g: (0,) * len(shape))

    return pl.pallas_call(
        prepare_kernel,
        grid=(1,),
        out_shape=[jax.ShapeDtypeStruct(*shape) for shape in shapes],
        in_specs=[whole(operand.shape) for operand in operands],
        out_specs=[whole(shape[0]) for shape in shapes],
        compiler_params=pltpu.CompilerParams(vmem_limit_bytes=56 * 1024 * 1024),
        cost_estimate=pl.CostEstimate(flops=500_000_000, bytes_accessed=16_000_000, transcendentals=0),
        name="prepare_tables",
    )(*operands)


def split_sum(total):
    high = total.astype(BF16).astype(F32)
    middle = (total - high).astype(BF16).astype(F32)
    return high, middle, total - high - middle


def complex_rows(beams):
    if beams % 2:
        return [(hyp, beam, None) for hyp in range(HYPS) for beam in range(beams)]
    return [(hyp, beam, beam + 1) for hyp in range(HYPS) for beam in range(0, beams, 2)]


def correlate_kernel(
    beams,
    segments,
    source_ref,
    interp_hbm,
    chosen_hbm,
    left_hbm,
    turn_hbm,
    right_hbm,
    spectrum_hbm,
    out_ref,
    interp_ref,
    chosen_ref,
    left_ref,
    turn_ref,
    right_ref,
    spectrum_ref,
    sems,
    next_ref,
    block_ref,
    column_ref,
    row_ref,
    wide_ref,
):
    fetches = [
        pltpu.make_async_copy(source, target, sems.at[index])
        for index, (source, target) in enumerate(
            (
                (interp_hbm, interp_ref),
                (chosen_hbm, chosen_ref),
                (left_hbm, left_ref),
                (turn_hbm, turn_ref),
                (right_hbm, right_ref),
                (spectrum_hbm, spectrum_ref),
            )
        )
    ]
    for fetch in fetches:
        fetch.start()
    get_interp, get_chosen, get_left, get_turn, get_right, get_spectrum = fetches
    points = turn_ref.shape[0]
    blocks = 2 * points
    lines = source_ref.shape[0]
    rows = complex_rows(beams)
    chunk = min(512, lines)

    get_interp.wait()
    for start in range(0, lines, chunk):
        next_ref[start : start + chunk, :] = dot(source_ref[start : start + chunk, :], interp_ref[BLOCK:, :])
    next_ref[lines : lines + 8, :] = next_ref[0:8, :]
    for start in range(0, lines, chunk):
        value = (
            dot(source_ref[start : start + chunk, :], interp_ref[:BLOCK, :])
            + next_ref[start + beams : start + beams + chunk, :]
        )
        for hyp in range(HYPS):
            block_ref[hyp, start : start + chunk, :] = value[:, hyp * BLOCK : (hyp + 1) * BLOCK]

    get_chosen.wait()
    for hyp in range(HYPS):
        warped = jnp.concatenate(
            [block_ref[hyp, pl.ds(beam, blocks, stride=beams), :].astype(BF16) for beam in range(beams)], axis=1
        )
        gathered = dot(chosen_ref[hyp * blocks : (hyp + 1) * blocks, :], warped).astype(BF16)
        for index, (row_hyp, *pair) in enumerate(rows):
            if row_hyp != hyp:
                continue
            for part, beam in enumerate(pair):
                for half in range(2):
                    lane = index * PAIR + half * BLOCK
                    target = (slice(part * points, (part + 1) * points), slice(lane, lane + BLOCK))
                    if beam is None:
                        column_ref[target] = jnp.zeros((points, BLOCK), BF16)
                    else:
                        column_ref[target] = gathered[
                            half * points : (half + 1) * points, beam * BLOCK : (beam + 1) * BLOCK
                        ]

    def left_product(index):
        both = dot(left_ref[...], column_ref[:, index * PAIR : (index + 1) * PAIR])
        value = both[: 2 * points] + both[2 * points :]
        return value[:points], value[points:]

    def right_product():
        value = row_ref[...]
        wide_ref[...] = dot(value, right_ref[: 2 * PAIR, :]) + dot(value, right_ref[2 * PAIR :, :])

    get_left.wait()
    get_turn.wait()
    turn_re, turn_im = turn_ref[:, :PAIR], turn_ref[:, PAIR:]
    for index in range(len(rows)):
        real, imag = left_product(index)
        place = slice(index * points, (index + 1) * points)
        row_ref[place, :PAIR] = (real * turn_re - imag * turn_im).astype(BF16)
        row_ref[place, PAIR:] = (real * turn_im + imag * turn_re).astype(BF16)
    get_right.wait()
    right_product()
    get_spectrum.wait()
    spectrum_re, spectrum_im = spectrum_ref[:, :PAIR], spectrum_ref[:, PAIR:]
    for index in range(len(rows)):
        place = slice(index * points, (index + 1) * points)
        real, imag = wide_ref[place, :PAIR], wide_ref[place, PAIR:]
        row_ref[place, PAIR:] = (real * spectrum_re - imag * spectrum_im).astype(BF16)
        row_ref[place, :PAIR] = (real * spectrum_im + imag * spectrum_re).astype(BF16)
    right_product()
    for index in range(len(rows)):
        place = slice(index * points, (index + 1) * points)
        lanes = slice(index * PAIR, (index + 1) * PAIR)
        imag, real = wide_ref[place, :PAIR], wide_ref[place, PAIR:]
        column_ref[points:, lanes] = (real * turn_re + imag * turn_im).astype(BF16)
        column_ref[:points, lanes] = (imag * turn_re - real * turn_im).astype(BF16)

    share = points // segments
    sums = [jnp.zeros((8, PAIR), F32) for _ in range(HYPS)]
    for index, (hyp, real_beam, imag_beam) in enumerate(rows):
        imag, real = left_product(index)
        for beam, value in ((real_beam, real), (imag_beam, imag)):
            if beam is None:
                continue
            power = value * value
            sums[hyp] = sums[hyp] + jnp.sum(power.reshape(points // 8, 8, PAIR), axis=0)
            first = (hyp * beams + beam) * 2 * share
            for segment in range(segments):
                piece = power[segment * share : (segment + 1) * share, :]
                out_ref[segment, first : first + 2 * share, :] = jnp.concatenate(
                    [piece[:, :BLOCK], piece[:, BLOCK:]], axis=0
                ).astype(BF16)
    place = lax.broadcasted_iota(jnp.int32, (16, BLOCK), 0)
    tail = jnp.zeros((16, BLOCK), F32)
    for hyp in range(HYPS):
        total = jnp.sum(jnp.sum(sums[hyp], axis=1, keepdims=True), axis=0, keepdims=True)
        for index, piece in enumerate(split_sum(total)):
            tail = jnp.where(place == hyp * 3 + index, piece, tail)
    tail = tail.astype(BF16)
    for segment in range(segments):
        out_ref[segment, HYPS * beams * 2 * share :, :] = tail


def correlate(source, interp, chosen, spectrum, tables, beams, segments):
    left, right, turn = tables
    points = turn.shape[0]
    lines = source.shape[0]
    count = len(complex_rows(beams))
    fetched = (interp, chosen, left, turn, right, spectrum)
    out_rows = HYPS * beams * 2 * (points // segments) + 16
    return pl.pallas_call(
        functools.partial(correlate_kernel, beams, segments),
        out_shape=jax.ShapeDtypeStruct((segments, out_rows, BLOCK), BF16),
        in_specs=[VMEM] + [ANY] * len(fetched),
        out_specs=VMEM,
        scratch_shapes=[pltpu.VMEM(array.shape, array.dtype) for array in fetched]
        + [
            pltpu.SemaphoreType.DMA((len(fetched),)),
            pltpu.VMEM((lines + 8, PAIR), F32),
            pltpu.VMEM((HYPS, lines, BLOCK), F32),
            pltpu.VMEM((2 * points, count * PAIR), BF16),
            pltpu.VMEM((count * points, 2 * PAIR), BF16),
            pltpu.VMEM((count * points, 2 * PAIR), F32),
        ],
        compiler_params=pltpu.CompilerParams(vmem_limit_bytes=56 * 1024 * 1024),
        cost_estimate=pl.CostEstimate(flops=4_000_000_000, bytes_accessed=6_000_000, transcendentals=0),
        name="warp_correlate",
    )(source, *fetched)


def finish_kernel(count, power_ref, sums_ref, out_ref, scratch_ref):
    hyp = pl.program_id(0)
    sums = sums_ref[...].astype(F32)
    place = lax.broadcasted_iota(jnp.int32, sums.shape, 1)
    picked = jnp.where((place >= 3 * hyp) & (place < 3 * hyp + 3), sums, 0.0)
    total = jnp.sum(jnp.sum(picked, axis=0), axis=0, keepdims=True)
    inverse = 1.0 / (total / count + 1e-06)
    devices, lines, _ = power_ref.shape
    for device in range(devices):
        scratch_ref[device * lines : (device + 1) * lines, :] = power_ref[device].astype(F32) * inverse
    beams = out_ref.shape[1]
    step = devices * lines // beams
    for line in range(step):
        half, block = divmod(line, step // 2)
        lane = block * PAIR + half * BLOCK
        out_ref[0, :, lane : lane + BLOCK] = scratch_ref[pl.ds(line, beams, stride=step), :].astype(BF16)


def finish(received, count, beams):
    segments, out_rows, _ = received.shape
    lines = (out_rows - 16) // HYPS
    samples = lines // beams * BLOCK
    return pl.pallas_call(
        functools.partial(finish_kernel, count),
        grid=(HYPS,),
        out_shape=jax.ShapeDtypeStruct((HYPS, segments * beams, samples), BF16),
        in_specs=[
            pl.BlockSpec((segments, lines, BLOCK), lambda g: (0, g, 0)),
            pl.BlockSpec((segments, 16, BLOCK), lambda g: (0, HYPS * lines // 16, 0)),
        ],
        out_specs=pl.BlockSpec((1, segments * beams, samples), lambda g: (g, 0, 0)),
        scratch_shapes=[pltpu.VMEM((segments * lines, BLOCK), F32)],
        cost_estimate=pl.CostEstimate(flops=1_000_000, bytes_accessed=1_200_000, transcendentals=0),
        name="scale_power",
    )(received, received)


def body(signal, warp_blocks, taps, tap_weights, replica):
    segments = lax.axis_size("tm")
    beams = signal.shape[0] // segments
    samples = signal.shape[1] * segments
    received = lax.all_to_all(spread(signal, segments), "tm", split_axis=0, concat_axis=0, tiled=True)
    tables = transform_tables(samples // PAIR)
    interp, chosen, spectrum = prepare(replica, taps, tap_weights, warp_blocks, tables)
    sent = correlate(received.reshape(-1, BLOCK), interp, chosen, spectrum, tables, beams, segments)
    back = lax.all_to_all(sent, "tm", split_axis=0, concat_axis=0, tiled=True)
    return finish(back, float(BEAMS * samples), beams)


def solution(mesh):
    in_specs = (
        P("groups", "tm"),
        P("groups", None),
        P("groups", None, None),
        P("groups", None, None),
        P(),
    )
    out_specs = P("groups", None, "tm")
    return jax.shard_map(body, mesh=mesh, in_specs=in_specs, out_specs=out_specs, check_vma=False)
```

```python
import functools
import math

import jax
import jax.numpy as jnp
import numpy as np
from jax import lax
from jax.experimental import pallas as pl
from jax.experimental.pallas import tpu as pltpu
from jax.sharding import PartitionSpec as P

BEAMS = 64
BLOCK = 128
PAIR = 2 * BLOCK
TAPS = 8
REPLICA = 16384
HYPS = 2
F32 = jnp.float32
BF16 = jnp.bfloat16
VMEM = pl.BlockSpec(memory_space=pltpu.VMEM)
SMEM = pl.BlockSpec(memory_space=pltpu.SMEM)
ANY = pl.BlockSpec(memory_space=pl.ANY)


def transform_tables(points):
    k, p = np.arange(points)[:, None], np.arange(points)[None, :]
    angle = 2.0 * math.pi * (k * p % points) / points
    cos, sin = np.cos(angle), np.sin(angle)
    left = np.block([[cos, sin], [-sin, cos]]).astype(np.float32)
    k, p = np.arange(PAIR)[:, None], np.arange(PAIR)[None, :]
    angle = 2.0 * math.pi * (k * p % PAIR) / PAIR
    cos, sin = np.cos(angle), np.sin(angle)
    right = np.block([[cos, -sin], [sin, cos]]).astype(np.float32)
    k, q = np.arange(points)[:, None], np.arange(PAIR)[None, :]
    angle = 2.0 * math.pi * (k * q) / (points * PAIR)
    turn = np.concatenate([np.cos(angle), -np.sin(angle)], axis=1).astype(np.float32)
    parts = []
    for table in (left, right):
        high = table.astype(jnp.bfloat16)
        low = (table - high.astype(np.float32)).astype(jnp.bfloat16)
        parts.append(np.concatenate([high, low], axis=0))
    return jnp.asarray(parts[0]), jnp.asarray(parts[1]), jnp.asarray(turn)


def split(value):
    high = value.astype(BF16)
    return high, (value - high.astype(F32)).astype(BF16)


def dot(left, right):
    return jnp.dot(left, right, preferred_element_type=F32)


def spread_kernel(signal_ref, out_ref):
    upper = lax.broadcasted_iota(jnp.int32, (8, BLOCK), 0) < 4
    groups, blocks = signal_ref.shape[0] // 16, signal_ref.shape[1] // BLOCK
    for group in range(groups):
        for quad in range(0, blocks, 4):
            tiles = []
            for block in range(quad, quad + 4):
                value = signal_ref[group * 16 : group * 16 + 16, block * BLOCK : (block + 1) * BLOCK].astype(F32)
                tiles.append((value[:8], value[8:]))
            for half in range(2):
                parts = [tile[half] for tile in tiles]
                turned = [pltpu.roll(part, 4, 0) for part in parts]
                first = [jnp.where(upper, parts[d], turned[d + 1]) for d in (0, 2)]
                second = [jnp.where(upper, turned[d], parts[d + 1]) for d in (0, 2)]
                device = group * 4 + half * 2
                rows = slice(quad * 4, quad * 4 + 16)
                out_ref[device, rows, :] = jnp.concatenate(first, axis=0).astype(BF16)
                out_ref[device + 1, rows, :] = jnp.concatenate(second, axis=0).astype(BF16)


def spread(signal, segments):
    beams, blocks = signal.shape[0] // segments, signal.shape[1] // BLOCK
    if beams != 4 or signal.shape[0] % 16 or blocks % 4:
        send = signal.reshape(segments, beams, blocks, BLOCK).transpose(0, 2, 1, 3)
        return send.reshape(segments, blocks * beams, BLOCK)
    return pl.pallas_call(
        spread_kernel,
        out_shape=jax.ShapeDtypeStruct((segments, blocks * beams, BLOCK), BF16),
        in_specs=[VMEM],
        out_specs=VMEM,
        name="spread_beams",
    )(signal)


def prepare_kernel(replica_ref, taps_ref, weights_ref, sources_ref, left_ref, right_ref, turn_ref, interp_ref, chosen_ref, spectrum_ref):
    window = lax.broadcasted_iota(jnp.int32, (PAIR, BLOCK), 0)
    for hyp in range(HYPS):
        total = jnp.zeros((PAIR, BLOCK), F32)
        for tap in range(TAPS):
            hit = taps_ref[hyp, tap : tap + 1, :] == window
            total = total + jnp.where(hit, weights_ref[hyp, tap : tap + 1, :], 0.0)
        interp_ref[:, hyp * BLOCK : (hyp + 1) * BLOCK] = total.astype(BF16)

    blocks = chosen_ref.shape[1]
    column = lax.broadcasted_iota(jnp.int32, (blocks, blocks), 1)
    for hyp in range(HYPS):
        rows = slice(hyp * blocks, (hyp + 1) * blocks)
        chosen_ref[rows, :] = (sources_ref[rows, :] == column).astype(F32).astype(BF16)

    points = turn_ref.shape[0]
    lines = replica_ref.shape[0]
    high, low = split(replica_ref[...])
    both = dot(left_ref[:, :lines], high)
    value = both[: 2 * points] + both[2 * points :] + dot(left_ref[: 2 * points, :lines], low)
    value_re, value_im = value[:points], value[points:]
    turn_re, turn_im = turn_ref[:, :PAIR], turn_ref[:, PAIR:]
    turned = jnp.concatenate(
        [value_re * turn_re - value_im * turn_im, value_re * turn_im + value_im * turn_re], axis=1
    )
    high, low = split(turned)
    upper, lower = right_ref[: 2 * PAIR, :], right_ref[2 * PAIR :, :]
    value = (dot(high, upper) + dot(high, lower) + dot(low, upper)) * (1.0 / (points * PAIR))
    spectrum_ref[:, :PAIR] = value[:, :PAIR]
    spectrum_ref[:, PAIR:] = -value[:, PAIR:]


def prepare(replica, taps, tap_weights, warp_blocks, tables):
    blocks = warp_blocks.shape[1]
    points = blocks // 2
    ordered = warp_blocks.reshape(HYPS, points, 2).transpose(0, 2, 1).reshape(HYPS * blocks, 1)
    operands = (replica.reshape(-1, PAIR), taps.transpose(0, 2, 1), tap_weights.transpose(0, 2, 1), ordered, *tables)
    shapes = ((PAIR, HYPS * BLOCK), BF16), ((HYPS * blocks, blocks), BF16), ((points, 2 * PAIR), F32)

    def whole(shape):
        return pl.BlockSpec(shape, lambda g: (0,) * len(shape))

    return pl.pallas_call(
        prepare_kernel,
        grid=(1,),
        out_shape=[jax.ShapeDtypeStruct(*shape) for shape in shapes],
        in_specs=[whole(operand.shape) for operand in operands],
        out_specs=[whole(shape[0]) for shape in shapes],
        compiler_params=pltpu.CompilerParams(vmem_limit_bytes=56 * 1024 * 1024),
        cost_estimate=pl.CostEstimate(flops=500_000_000, bytes_accessed=16_000_000, transcendentals=0),
        name="prepare_tables",
    )(*operands)


def split_sum(total):
    high = total.astype(BF16).astype(F32)
    middle = (total - high).astype(BF16).astype(F32)
    return high, middle, total - high - middle


def tail_of(totals):
    place = lax.broadcasted_iota(jnp.int32, (16, BLOCK), 0)
    tail = jnp.zeros((16, BLOCK), F32)
    for hyp, total in enumerate(totals):
        for index, piece in enumerate(split_sum(total)):
            tail = jnp.where(place == hyp * 3 + index, piece, tail)
    return tail.astype(BF16)


def totals_of(tails):
    place = lax.broadcasted_iota(jnp.int32, (16, BLOCK), 0)
    total = functools.reduce(jnp.add, [tail.astype(F32) for tail in tails])
    return [
        jnp.sum(jnp.where((place >= 3 * hyp) & (place < 3 * hyp + 3), total, 0.0), axis=0, keepdims=True)
        for hyp in range(HYPS)
    ]


def complex_rows(beams):
    if beams % 2:
        return [(hyp, beam, None) for hyp in range(HYPS) for beam in range(beams)]
    return [(hyp, beam, beam + 1) for hyp in range(HYPS) for beam in range(0, beams, 2)]


def correlate_kernel(
    beams,
    segments,
    paired,
    place_ref,
    source_ref,
    interp_hbm,
    chosen_hbm,
    left_hbm,
    turn_hbm,
    right_hbm,
    spectrum_hbm,
    *refs,
):
    out_refs, refs = refs[: 1 + paired], refs[1 + paired :]
    (
    interp_ref,
    chosen_ref,
    left_ref,
    turn_ref,
    right_ref,
    spectrum_ref,
    sems,
    next_ref,
    block_ref,
    column_ref,
    row_ref,
    wide_ref,
    ) = refs
    fetches = [
        pltpu.make_async_copy(source, target, sems.at[index])
        for index, (source, target) in enumerate(
            (
                (interp_hbm, interp_ref),
                (chosen_hbm, chosen_ref),
                (left_hbm, left_ref),
                (turn_hbm, turn_ref),
                (right_hbm, right_ref),
                (spectrum_hbm, spectrum_ref),
            )
        )
    ]
    for fetch in fetches:
        fetch.start()
    get_interp, get_chosen, get_left, get_turn, get_right, get_spectrum = fetches
    points = turn_ref.shape[0]
    blocks = 2 * points
    lines = source_ref.shape[0]
    rows = complex_rows(beams)
    chunk = min(512, lines)

    get_interp.wait()
    for start in range(0, lines, chunk):
        next_ref[start : start + chunk, :] = dot(source_ref[start : start + chunk, :], interp_ref[BLOCK:, :])
    next_ref[lines : lines + 8, :] = next_ref[0:8, :]
    for start in range(0, lines, chunk):
        value = (
            dot(source_ref[start : start + chunk, :], interp_ref[:BLOCK, :])
            + next_ref[start + beams : start + beams + chunk, :]
        )
        for hyp in range(HYPS):
            block_ref[hyp, start : start + chunk, :] = value[:, hyp * BLOCK : (hyp + 1) * BLOCK]

    get_chosen.wait()
    for hyp in range(HYPS):
        warped = jnp.concatenate(
            [block_ref[hyp, pl.ds(beam, blocks, stride=beams), :].astype(BF16) for beam in range(beams)], axis=1
        )
        gathered = dot(chosen_ref[hyp * blocks : (hyp + 1) * blocks, :], warped).astype(BF16)
        for index, (row_hyp, *pair) in enumerate(rows):
            if row_hyp != hyp:
                continue
            for part, beam in enumerate(pair):
                for half in range(2):
                    lane = index * PAIR + half * BLOCK
                    target = (slice(part * points, (part + 1) * points), slice(lane, lane + BLOCK))
                    if beam is None:
                        column_ref[target] = jnp.zeros((points, BLOCK), BF16)
                    else:
                        column_ref[target] = gathered[
                            half * points : (half + 1) * points, beam * BLOCK : (beam + 1) * BLOCK
                        ]

    def left_product(index):
        both = dot(left_ref[...], column_ref[:, index * PAIR : (index + 1) * PAIR])
        value = both[: 2 * points] + both[2 * points :]
        return value[:points], value[points:]

    def right_product():
        value = row_ref[...]
        wide_ref[...] = dot(value, right_ref[: 2 * PAIR, :]) + dot(value, right_ref[2 * PAIR :, :])

    get_left.wait()
    get_turn.wait()
    turn_re, turn_im = turn_ref[:, :PAIR], turn_ref[:, PAIR:]
    for index in range(len(rows)):
        real, imag = left_product(index)
        place = slice(index * points, (index + 1) * points)
        row_ref[place, :PAIR] = (real * turn_re - imag * turn_im).astype(BF16)
        row_ref[place, PAIR:] = (real * turn_im + imag * turn_re).astype(BF16)
    get_right.wait()
    right_product()
    get_spectrum.wait()
    spectrum_re, spectrum_im = spectrum_ref[:, :PAIR], spectrum_ref[:, PAIR:]
    for index in range(len(rows)):
        place = slice(index * points, (index + 1) * points)
        real, imag = wide_ref[place, :PAIR], wide_ref[place, PAIR:]
        row_ref[place, PAIR:] = (real * spectrum_re - imag * spectrum_im).astype(BF16)
        row_ref[place, :PAIR] = (real * spectrum_im + imag * spectrum_re).astype(BF16)
    right_product()
    for index in range(len(rows)):
        place = slice(index * points, (index + 1) * points)
        lanes = slice(index * PAIR, (index + 1) * PAIR)
        imag, real = wide_ref[place, :PAIR], wide_ref[place, PAIR:]
        column_ref[points:, lanes] = (real * turn_re + imag * turn_im).astype(BF16)
        column_ref[:points, lanes] = (imag * turn_re - real * turn_im).astype(BF16)

    share = points // segments
    sums = [jnp.zeros((8, PAIR), F32) for _ in range(HYPS)]
    for index, (hyp, real_beam, imag_beam) in enumerate(rows):
        imag, real = left_product(index)
        for beam, value in ((real_beam, real), (imag_beam, imag)):
            if beam is None:
                continue
            power = value * value
            sums[hyp] = sums[hyp] + jnp.sum(power.reshape(points // 8, 8, PAIR), axis=0)
            first = (hyp * beams + beam) * 2 * share
            pieces = [power[segment * share : (segment + 1) * share, :] for segment in range(segments)]
            pieces = [jnp.concatenate([piece[:, :BLOCK], piece[:, BLOCK:]], axis=0) for piece in pieces]
            if paired:
                is_even = place_ref[0] % 2 == 0
                for chip in range(segments // 2):
                    start = chip * HYPS * beams * 2 * share + first
                    even, odd = pieces[2 * chip], pieces[2 * chip + 1]
                    out_refs[0][start : start + 2 * share, :] = jnp.where(is_even, even, odd).astype(BF16)
                    out_refs[1][start : start + 2 * share, :] = jnp.where(is_even, odd, even).astype(BF16)
            else:
                for segment, piece in enumerate(pieces):
                    out_refs[0][segment, first : first + 2 * share, :] = piece.astype(BF16)
    tail = tail_of([jnp.sum(jnp.sum(value, axis=1, keepdims=True), axis=0, keepdims=True) for value in sums])
    if paired:
        for out_ref in out_refs:
            out_ref[out_ref.shape[0] - 16 :, :] = tail
    else:
        for segment in range(segments):
            out_refs[0][segment, HYPS * beams * 2 * share :, :] = tail


def correlate(place, source, interp, chosen, spectrum, tables, beams, segments, paired):
    left, right, turn = tables
    points = turn.shape[0]
    lines = source.shape[0]
    count = len(complex_rows(beams))
    fetched = (interp, chosen, left, turn, right, spectrum)
    out_rows = HYPS * beams * 2 * (points // segments) + 16
    if paired:
        shape = jax.ShapeDtypeStruct((segments // 2 * (out_rows - 16) + 16, BLOCK), BF16)
        out_shape, out_specs = (shape, shape), (VMEM, VMEM)
    else:
        out_shape, out_specs = jax.ShapeDtypeStruct((segments, out_rows, BLOCK), BF16), VMEM
    return pl.pallas_call(
        functools.partial(correlate_kernel, beams, segments, paired),
        out_shape=out_shape,
        in_specs=[SMEM, VMEM] + [ANY] * len(fetched),
        out_specs=out_specs,
        scratch_shapes=[pltpu.VMEM(array.shape, array.dtype) for array in fetched]
        + [
            pltpu.SemaphoreType.DMA((len(fetched),)),
            pltpu.VMEM((lines + 8, PAIR), F32),
            pltpu.VMEM((HYPS, lines, BLOCK), F32),
            pltpu.VMEM((2 * points, count * PAIR), BF16),
            pltpu.VMEM((count * points, 2 * PAIR), BF16),
            pltpu.VMEM((count * points, 2 * PAIR), F32),
        ],
        compiler_params=pltpu.CompilerParams(vmem_limit_bytes=56 * 1024 * 1024),
        cost_estimate=pl.CostEstimate(flops=4_000_000_000, bytes_accessed=6_000_000, transcendentals=0),
        name="warp_correlate",
    )(place, source, *fetched)


def finish_kernel(count, power_ref, sums_ref, out_ref, scratch_ref):
    hyp = pl.program_id(0)
    sums = sums_ref[...].astype(F32)
    place = lax.broadcasted_iota(jnp.int32, sums.shape, 1)
    picked = jnp.where((place >= 3 * hyp) & (place < 3 * hyp + 3), sums, 0.0)
    total = jnp.sum(jnp.sum(picked, axis=0), axis=0, keepdims=True)
    inverse = 1.0 / (total / count + 1e-06)
    devices, lines, _ = power_ref.shape
    for device in range(devices):
        scratch_ref[device * lines : (device + 1) * lines, :] = power_ref[device].astype(F32) * inverse
    beams = out_ref.shape[1]
    step = devices * lines // beams
    for line in range(step):
        half, block = divmod(line, step // 2)
        lane = block * PAIR + half * BLOCK
        out_ref[0, :, lane : lane + BLOCK] = scratch_ref[pl.ds(line, beams, stride=step), :].astype(BF16)


def finish(received, count, beams):
    segments, out_rows, _ = received.shape
    lines = (out_rows - 16) // HYPS
    samples = lines // beams * BLOCK
    return pl.pallas_call(
        functools.partial(finish_kernel, count),
        grid=(HYPS,),
        out_shape=jax.ShapeDtypeStruct((HYPS, segments * beams, samples), BF16),
        in_specs=[
            pl.BlockSpec((segments, lines, BLOCK), lambda g: (0, g, 0)),
            pl.BlockSpec((segments, 16, BLOCK), lambda g: (0, HYPS * lines // 16, 0)),
        ],
        out_specs=pl.BlockSpec((1, segments * beams, samples), lambda g: (g, 0, 0)),
        scratch_shapes=[pltpu.VMEM((segments * lines, BLOCK), F32)],
        cost_estimate=pl.CostEstimate(flops=1_000_000, bytes_accessed=1_200_000, transcendentals=0),
        name="scale_power",
    )(received, received)


def arrange_kernel(place_ref, mine_ref, got_ref, *out_refs):
    chip = place_ref[0] // 2
    count = len(out_refs)
    lines = (mine_ref.shape[0] - 16) // count
    tails = [ref[count * lines :, :] for ref in (mine_ref, got_ref)]
    tail = tail_of([total[:, :1] for total in totals_of(tails)])
    for offset, out_ref in enumerate(out_refs):
        rows = pl.ds(pl.multiple_of((chip ^ offset) * lines, lines), lines)
        out_ref[:lines, :] = mine_ref[rows, :]
        out_ref[lines : 2 * lines, :] = got_ref[rows, :]
        out_ref[2 * lines :, :] = tail


def arrange(place, mine, got, chips):
    lines = (mine.shape[0] - 16) // chips
    shape = jax.ShapeDtypeStruct((2 * lines + 16, BLOCK), BF16)
    return pl.pallas_call(
        arrange_kernel,
        out_shape=[shape] * chips,
        in_specs=[SMEM, VMEM, VMEM],
        out_specs=[VMEM] * chips,
        compiler_params=pltpu.CompilerParams(vmem_limit_bytes=16 * 1024 * 1024),
        cost_estimate=pl.CostEstimate(flops=1_000_000, bytes_accessed=1_200_000, transcendentals=0),
        name="arrange_chips",
    )(place, mine, got)


def join_kernel(count, place_ref, *refs):
    chunk_refs, out_ref, scratch_ref = refs[:-2], refs[-2], refs[-1]
    chip, core = place_ref[0] // 2, place_ref[0] % 2
    lines = chunk_refs[0].shape[0] - 16
    totals = totals_of([ref[lines:, :] for ref in chunk_refs])
    inverse = [1.0 / (total / count + 1e-06) for total in totals]
    run = lines // 2 // HYPS
    for offset, ref in enumerate(chunk_refs):
        for part in range(2):
            start = pl.multiple_of(((chip ^ offset) * 2 + (core ^ part)) * run, run)
            for hyp in range(HYPS):
                first = (part * HYPS + hyp) * run
                scratch_ref[hyp, pl.ds(start, run), :] = ref[first : first + run, :].astype(F32) * inverse[hyp]
    beams = out_ref.shape[1]
    step = scratch_ref.shape[1] // beams
    for hyp in range(HYPS):
        for line in range(step):
            half, block = divmod(line, step // 2)
            lane = block * PAIR + half * BLOCK
            out_ref[hyp, :, lane : lane + BLOCK] = scratch_ref[hyp, pl.ds(line, beams, stride=step), :].astype(BF16)


def join(place, chunks, count, beams):
    lines = chunks[0].shape[0] - 16
    rows = lines // HYPS * len(chunks)
    return pl.pallas_call(
        functools.partial(join_kernel, count),
        out_shape=jax.ShapeDtypeStruct((HYPS, beams, rows // beams * BLOCK), BF16),
        in_specs=[SMEM] + [VMEM] * len(chunks),
        out_specs=VMEM,
        scratch_shapes=[pltpu.VMEM((HYPS, rows, BLOCK), F32)],
        compiler_params=pltpu.CompilerParams(vmem_limit_bytes=16 * 1024 * 1024),
        cost_estimate=pl.CostEstimate(flops=1_000_000, bytes_accessed=1_200_000, transcendentals=0),
        name="scale_power",
    )(place, *chunks)


def exchange(value, offset, segments):
    return lax.ppermute(value, "tm", [(index, index ^ offset) for index in range(segments)])


def body(signal, warp_blocks, taps, tap_weights, replica):
    segments = lax.axis_size("tm")
    beams = signal.shape[0] // segments
    samples = signal.shape[1] * segments
    count = float(BEAMS * samples)
    paired = segments == 16
    place = lax.axis_index("tm").astype(jnp.int32).reshape(1)
    received = lax.all_to_all(spread(signal, segments), "tm", split_axis=0, concat_axis=0, tiled=True)
    tables = transform_tables(samples // PAIR)
    interp, chosen, spectrum = prepare(replica, taps, tap_weights, warp_blocks, tables)
    sent = correlate(
        place, received.reshape(-1, BLOCK), interp, chosen, spectrum, tables, beams, segments, paired
    )
    if not paired:
        back = lax.all_to_all(sent, "tm", split_axis=0, concat_axis=0, tiled=True)
        return finish(back, count, beams)
    mine, theirs = sent
    chips = segments // 2
    chunks = arrange(place, mine, exchange(theirs, 1, segments), chips)
    order = [offset for offset in (5, 4, 7, 6, 3, 2, 1) if offset < chips]
    arrived = {offset: exchange(chunks[offset], 2 * offset, segments) for offset in order}
    arrived[0] = chunks[0]
    return join(place, [arrived[offset] for offset in range(chips)], count, signal.shape[0])


def solution(mesh):
    in_specs = (
        P("groups", "tm"),
        P("groups", None),
        P("groups", None, None),
        P("groups", None, None),
        P(),
    )
    out_specs = P("groups", None, "tm")
    return jax.shard_map(body, mesh=mesh, in_specs=in_specs, out_specs=out_specs, check_vma=False)
```

```python
import functools
import math

import jax
import jax.numpy as jnp
import numpy as np
from jax import lax
from jax.experimental import pallas as pl
from jax.experimental.pallas import tpu as pltpu
from jax.sharding import PartitionSpec as P

BEAMS = 64
BLOCK = 128
PAIR = 2 * BLOCK
TAPS = 8
REPLICA = 16384
HYPS = 2
F32 = jnp.float32
BF16 = jnp.bfloat16
VMEM = pl.BlockSpec(memory_space=pltpu.VMEM)
SMEM = pl.BlockSpec(memory_space=pltpu.SMEM)
ANY = pl.BlockSpec(memory_space=pl.ANY)


def transform_tables(points):
    k, p = np.arange(points)[:, None], np.arange(points)[None, :]
    angle = 2.0 * math.pi * (k * p % points) / points
    cos, sin = np.cos(angle), np.sin(angle)
    left = np.block([[cos, sin], [-sin, cos]]).astype(np.float32)
    k, p = np.arange(PAIR)[:, None], np.arange(PAIR)[None, :]
    angle = 2.0 * math.pi * (k * p % PAIR) / PAIR
    cos, sin = np.cos(angle), np.sin(angle)
    right = np.block([[cos, -sin], [sin, cos]]).astype(np.float32)
    k, q = np.arange(points)[:, None], np.arange(PAIR)[None, :]
    angle = 2.0 * math.pi * (k * q) / (points * PAIR)
    turn = np.concatenate([np.cos(angle), -np.sin(angle)], axis=1).astype(np.float32)
    parts = []
    for table in (left, right):
        high = table.astype(jnp.bfloat16)
        low = (table - high.astype(np.float32)).astype(jnp.bfloat16)
        parts.append(np.concatenate([high, low], axis=0))
    return jnp.asarray(parts[0]), jnp.asarray(parts[1]), jnp.asarray(turn)


def split(value):
    high = value.astype(BF16)
    return high, (value - high.astype(F32)).astype(BF16)


def dot(left, right):
    return jnp.dot(left, right, preferred_element_type=F32)


def spread_kernel(signal_ref, out_ref):
    upper = lax.broadcasted_iota(jnp.int32, (8, BLOCK), 0) < 4
    groups, blocks = signal_ref.shape[0] // 16, signal_ref.shape[1] // BLOCK
    for group in range(groups):
        for quad in range(0, blocks, 4):
            tiles = []
            for block in range(quad, quad + 4):
                value = signal_ref[group * 16 : group * 16 + 16, block * BLOCK : (block + 1) * BLOCK].astype(F32)
                tiles.append((value[:8], value[8:]))
            for half in range(2):
                parts = [tile[half] for tile in tiles]
                turned = [pltpu.roll(part, 4, 0) for part in parts]
                first = [jnp.where(upper, parts[d], turned[d + 1]) for d in (0, 2)]
                second = [jnp.where(upper, turned[d], parts[d + 1]) for d in (0, 2)]
                device = group * 4 + half * 2
                rows = slice(quad * 4, quad * 4 + 16)
                out_ref[device, rows, :] = jnp.concatenate(first, axis=0).astype(BF16)
                out_ref[device + 1, rows, :] = jnp.concatenate(second, axis=0).astype(BF16)


def spread(signal, segments):
    beams, blocks = signal.shape[0] // segments, signal.shape[1] // BLOCK
    if beams != 4 or signal.shape[0] % 16 or blocks % 4:
        send = signal.reshape(segments, beams, blocks, BLOCK).transpose(0, 2, 1, 3)
        return send.reshape(segments, blocks * beams, BLOCK)
    return pl.pallas_call(
        spread_kernel,
        out_shape=jax.ShapeDtypeStruct((segments, blocks * beams, BLOCK), BF16),
        in_specs=[VMEM],
        out_specs=VMEM,
        name="spread_beams",
    )(signal)


def prepare_kernel(replica_ref, taps_ref, weights_ref, sources_ref, left_ref, right_ref, turn_ref, interp_ref, chosen_ref, spectrum_ref):
    window = lax.broadcasted_iota(jnp.int32, (PAIR, BLOCK), 0)
    for hyp in range(HYPS):
        total = jnp.zeros((PAIR, BLOCK), F32)
        for tap in range(TAPS):
            hit = taps_ref[hyp, tap : tap + 1, :] == window
            total = total + jnp.where(hit, weights_ref[hyp, tap : tap + 1, :], 0.0)
        interp_ref[:, hyp * BLOCK : (hyp + 1) * BLOCK] = total.astype(BF16)

    blocks = chosen_ref.shape[1]
    column = lax.broadcasted_iota(jnp.int32, (blocks, blocks), 1)
    for hyp in range(HYPS):
        rows = slice(hyp * blocks, (hyp + 1) * blocks)
        chosen_ref[rows, :] = (sources_ref[rows, :] == column).astype(F32).astype(BF16)

    points = turn_ref.shape[0]
    lines = replica_ref.shape[0]
    high, low = split(replica_ref[...])
    both = dot(left_ref[:, :lines], high)
    value = both[: 2 * points] + both[2 * points :] + dot(left_ref[: 2 * points, :lines], low)
    value_re, value_im = value[:points], value[points:]
    turn_re, turn_im = turn_ref[:, :PAIR], turn_ref[:, PAIR:]
    turned = jnp.concatenate(
        [value_re * turn_re - value_im * turn_im, value_re * turn_im + value_im * turn_re], axis=1
    )
    high, low = split(turned)
    upper, lower = right_ref[: 2 * PAIR, :], right_ref[2 * PAIR :, :]
    value = (dot(high, upper) + dot(high, lower) + dot(low, upper)) * (1.0 / (points * PAIR))
    spectrum_ref[:, :PAIR] = value[:, :PAIR]
    spectrum_ref[:, PAIR:] = -value[:, PAIR:]


def prepare(replica, taps, tap_weights, warp_blocks, tables):
    blocks = warp_blocks.shape[1]
    points = blocks // 2
    ordered = warp_blocks.reshape(HYPS, points, 2).transpose(0, 2, 1).reshape(HYPS * blocks, 1)
    operands = (replica.reshape(-1, PAIR), taps.transpose(0, 2, 1), tap_weights.transpose(0, 2, 1), ordered, *tables)
    shapes = ((PAIR, HYPS * BLOCK), BF16), ((HYPS * blocks, blocks), BF16), ((points, 2 * PAIR), F32)

    def whole(shape):
        return pl.BlockSpec(shape, lambda g: (0,) * len(shape))

    return pl.pallas_call(
        prepare_kernel,
        grid=(1,),
        out_shape=[jax.ShapeDtypeStruct(*shape) for shape in shapes],
        in_specs=[whole(operand.shape) for operand in operands],
        out_specs=[VMEM] * len(shapes),
        compiler_params=pltpu.CompilerParams(vmem_limit_bytes=24 * 1024 * 1024),
        cost_estimate=pl.CostEstimate(flops=500_000_000, bytes_accessed=16_000_000, transcendentals=0),
        name="prepare_tables",
    )(*operands)


def split_sum(total):
    high = total.astype(BF16).astype(F32)
    middle = (total - high).astype(BF16).astype(F32)
    return high, middle, total - high - middle


def tail_of(totals):
    place = lax.broadcasted_iota(jnp.int32, (16, BLOCK), 0)
    tail = jnp.zeros((16, BLOCK), F32)
    for hyp, total in enumerate(totals):
        for index, piece in enumerate(split_sum(total)):
            tail = jnp.where(place == hyp * 3 + index, piece, tail)
    return tail.astype(BF16)


def totals_of(tails):
    place = lax.broadcasted_iota(jnp.int32, (16, BLOCK), 0)
    total = functools.reduce(jnp.add, [tail.astype(F32) for tail in tails])
    return [
        jnp.sum(jnp.where((place >= 3 * hyp) & (place < 3 * hyp + 3), total, 0.0), axis=0, keepdims=True)
        for hyp in range(HYPS)
    ]


def complex_rows(beams):
    if beams % 2:
        return [(hyp, beam, None) for hyp in range(HYPS) for beam in range(beams)]
    return [(hyp, beam, beam + 1) for hyp in range(HYPS) for beam in range(0, beams, 2)]


def correlate_kernel(
    beams,
    segments,
    paired,
    place_ref,
    source_ref,
    interp_hbm,
    chosen_hbm,
    left_hbm,
    turn_hbm,
    right_hbm,
    spectrum_hbm,
    *refs,
):
    out_refs, refs = refs[: 1 + paired], refs[1 + paired :]
    (
    interp_ref,
    chosen_ref,
    left_ref,
    turn_ref,
    right_ref,
    spectrum_ref,
    sems,
    next_ref,
    block_ref,
    column_ref,
    row_ref,
    wide_ref,
    ) = refs
    fetches = [
        pltpu.make_async_copy(source, target, sems.at[index])
        for index, (source, target) in enumerate(
            (
                (interp_hbm, interp_ref),
                (chosen_hbm, chosen_ref),
                (left_hbm, left_ref),
                (turn_hbm, turn_ref),
                (right_hbm, right_ref),
                (spectrum_hbm, spectrum_ref),
            )
        )
    ]
    for fetch in fetches:
        fetch.start()
    get_interp, get_chosen, get_left, get_turn, get_right, get_spectrum = fetches
    points = turn_ref.shape[0]
    blocks = 2 * points
    lines = source_ref.shape[0]
    rows = complex_rows(beams)
    chunk = min(512, lines)

    get_interp.wait()
    for start in range(0, lines, chunk):
        next_ref[start : start + chunk, :] = dot(source_ref[start : start + chunk, :], interp_ref[BLOCK:, :])
    next_ref[lines : lines + 8, :] = next_ref[0:8, :]
    for start in range(0, lines, chunk):
        value = (
            dot(source_ref[start : start + chunk, :], interp_ref[:BLOCK, :])
            + next_ref[start + beams : start + beams + chunk, :]
        )
        for hyp in range(HYPS):
            block_ref[hyp, start : start + chunk, :] = value[:, hyp * BLOCK : (hyp + 1) * BLOCK]

    get_chosen.wait()
    for hyp in range(HYPS):
        warped = jnp.concatenate(
            [block_ref[hyp, pl.ds(beam, blocks, stride=beams), :].astype(BF16) for beam in range(beams)], axis=1
        )
        gathered = dot(chosen_ref[hyp * blocks : (hyp + 1) * blocks, :], warped).astype(BF16)
        for index, (row_hyp, *pair) in enumerate(rows):
            if row_hyp != hyp:
                continue
            for part, beam in enumerate(pair):
                for half in range(2):
                    lane = index * PAIR + half * BLOCK
                    target = (slice(part * points, (part + 1) * points), slice(lane, lane + BLOCK))
                    if beam is None:
                        column_ref[target] = jnp.zeros((points, BLOCK), BF16)
                    else:
                        column_ref[target] = gathered[
                            half * points : (half + 1) * points, beam * BLOCK : (beam + 1) * BLOCK
                        ]

    def left_product(index):
        both = dot(left_ref[...], column_ref[:, index * PAIR : (index + 1) * PAIR])
        value = both[: 2 * points] + both[2 * points :]
        return value[:points], value[points:]

    def right_product():
        value = row_ref[...]
        wide_ref[...] = dot(value, right_ref[: 2 * PAIR, :]) + dot(value, right_ref[2 * PAIR :, :])

    get_left.wait()
    get_turn.wait()
    turn_re, turn_im = turn_ref[:, :PAIR], turn_ref[:, PAIR:]
    for index in range(len(rows)):
        real, imag = left_product(index)
        place = slice(index * points, (index + 1) * points)
        row_ref[place, :PAIR] = (real * turn_re - imag * turn_im).astype(BF16)
        row_ref[place, PAIR:] = (real * turn_im + imag * turn_re).astype(BF16)
    get_right.wait()
    right_product()
    get_spectrum.wait()
    spectrum_re, spectrum_im = spectrum_ref[:, :PAIR], spectrum_ref[:, PAIR:]
    for index in range(len(rows)):
        place = slice(index * points, (index + 1) * points)
        real, imag = wide_ref[place, :PAIR], wide_ref[place, PAIR:]
        row_ref[place, PAIR:] = (real * spectrum_re - imag * spectrum_im).astype(BF16)
        row_ref[place, :PAIR] = (real * spectrum_im + imag * spectrum_re).astype(BF16)
    right_product()
    for index in range(len(rows)):
        place = slice(index * points, (index + 1) * points)
        lanes = slice(index * PAIR, (index + 1) * PAIR)
        imag, real = wide_ref[place, :PAIR], wide_ref[place, PAIR:]
        column_ref[points:, lanes] = (real * turn_re + imag * turn_im).astype(BF16)
        column_ref[:points, lanes] = (imag * turn_re - real * turn_im).astype(BF16)

    share = points // segments
    sums = [jnp.zeros((8, PAIR), F32) for _ in range(HYPS)]
    for index, (hyp, real_beam, imag_beam) in enumerate(rows):
        imag, real = left_product(index)
        for beam, value in ((real_beam, real), (imag_beam, imag)):
            if beam is None:
                continue
            power = value * value
            sums[hyp] = sums[hyp] + jnp.sum(power.reshape(points // 8, 8, PAIR), axis=0)
            first = (hyp * beams + beam) * 2 * share
            pieces = [power[segment * share : (segment + 1) * share, :] for segment in range(segments)]
            pieces = [jnp.concatenate([piece[:, :BLOCK], piece[:, BLOCK:]], axis=0) for piece in pieces]
            if paired:
                is_even = place_ref[0] % 2 == 0
                for chip in range(segments // 2):
                    start = chip * HYPS * beams * 2 * share + first
                    even, odd = pieces[2 * chip], pieces[2 * chip + 1]
                    out_refs[0][start : start + 2 * share, :] = jnp.where(is_even, even, odd).astype(BF16)
                    out_refs[1][start : start + 2 * share, :] = jnp.where(is_even, odd, even).astype(BF16)
            else:
                for segment, piece in enumerate(pieces):
                    out_refs[0][segment, first : first + 2 * share, :] = piece.astype(BF16)
    tail = tail_of([jnp.sum(jnp.sum(value, axis=1, keepdims=True), axis=0, keepdims=True) for value in sums])
    if paired:
        for out_ref in out_refs:
            out_ref[out_ref.shape[0] - 16 :, :] = tail
    else:
        for segment in range(segments):
            out_refs[0][segment, HYPS * beams * 2 * share :, :] = tail


def correlate(place, source, interp, chosen, spectrum, tables, beams, segments, paired):
    left, right, turn = tables
    points = turn.shape[0]
    lines = source.shape[0]
    count = len(complex_rows(beams))
    fetched = (interp, chosen, left, turn, right, spectrum)
    out_rows = HYPS * beams * 2 * (points // segments) + 16
    if paired:
        shape = jax.ShapeDtypeStruct((segments // 2 * (out_rows - 16) + 16, BLOCK), BF16)
        out_shape, out_specs = (shape, shape), (VMEM, VMEM)
    else:
        out_shape, out_specs = jax.ShapeDtypeStruct((segments, out_rows, BLOCK), BF16), VMEM
    return pl.pallas_call(
        functools.partial(correlate_kernel, beams, segments, paired),
        out_shape=out_shape,
        in_specs=[SMEM, VMEM] + [ANY] * len(fetched),
        out_specs=out_specs,
        scratch_shapes=[pltpu.VMEM(array.shape, array.dtype) for array in fetched]
        + [
            pltpu.SemaphoreType.DMA((len(fetched),)),
            pltpu.VMEM((lines + 8, PAIR), F32),
            pltpu.VMEM((HYPS, lines, BLOCK), F32),
            pltpu.VMEM((2 * points, count * PAIR), BF16),
            pltpu.VMEM((count * points, 2 * PAIR), BF16),
            pltpu.VMEM((count * points, 2 * PAIR), F32),
        ],
        compiler_params=pltpu.CompilerParams(vmem_limit_bytes=24 * 1024 * 1024),
        cost_estimate=pl.CostEstimate(flops=4_000_000_000, bytes_accessed=6_000_000, transcendentals=0),
        name="warp_correlate",
    )(place, source, *fetched)


def finish_kernel(count, power_ref, sums_ref, out_ref, scratch_ref):
    hyp = pl.program_id(0)
    sums = sums_ref[...].astype(F32)
    place = lax.broadcasted_iota(jnp.int32, sums.shape, 1)
    picked = jnp.where((place >= 3 * hyp) & (place < 3 * hyp + 3), sums, 0.0)
    total = jnp.sum(jnp.sum(picked, axis=0), axis=0, keepdims=True)
    inverse = 1.0 / (total / count + 1e-06)
    devices, lines, _ = power_ref.shape
    for device in range(devices):
        scratch_ref[device * lines : (device + 1) * lines, :] = power_ref[device].astype(F32) * inverse
    beams = out_ref.shape[1]
    step = devices * lines // beams
    for line in range(step):
        half, block = divmod(line, step // 2)
        lane = block * PAIR + half * BLOCK
        out_ref[0, :, lane : lane + BLOCK] = scratch_ref[pl.ds(line, beams, stride=step), :].astype(BF16)


def finish(received, count, beams):
    segments, out_rows, _ = received.shape
    lines = (out_rows - 16) // HYPS
    samples = lines // beams * BLOCK
    return pl.pallas_call(
        functools.partial(finish_kernel, count),
        grid=(HYPS,),
        out_shape=jax.ShapeDtypeStruct((HYPS, segments * beams, samples), BF16),
        in_specs=[
            pl.BlockSpec((segments, lines, BLOCK), lambda g: (0, g, 0)),
            pl.BlockSpec((segments, 16, BLOCK), lambda g: (0, HYPS * lines // 16, 0)),
        ],
        out_specs=pl.BlockSpec((1, segments * beams, samples), lambda g: (g, 0, 0)),
        scratch_shapes=[pltpu.VMEM((segments * lines, BLOCK), F32)],
        cost_estimate=pl.CostEstimate(flops=1_000_000, bytes_accessed=1_200_000, transcendentals=0),
        name="scale_power",
    )(received, received)


def chip_order(chips):
    far, near = range(chips // 2, chips), [*range(1, chips // 2), 0]
    return [offset for pair in zip(far, near) for offset in pair][:-1] + [0]


def arrange_kernel(place_ref, mine_ref, got_ref, *out_refs):
    chip = place_ref[0] // 2
    count = len(out_refs)
    lines = (mine_ref.shape[0] - 16) // count
    tails = [ref[count * lines :, :] for ref in (mine_ref, got_ref)]
    tail = tail_of([total[:, :1] for total in totals_of(tails)])
    for offset, out_ref in zip(chip_order(count), out_refs):
        rows = pl.ds(pl.multiple_of((chip ^ offset) * lines, lines), lines)
        out_ref[:lines, :] = mine_ref[rows, :]
        out_ref[lines : 2 * lines, :] = got_ref[rows, :]
        out_ref[2 * lines :, :] = tail


def arrange(place, mine, got, chips):
    lines = (mine.shape[0] - 16) // chips
    shape = jax.ShapeDtypeStruct((2 * lines + 16, BLOCK), BF16)
    return pl.pallas_call(
        arrange_kernel,
        out_shape=[shape] * chips,
        in_specs=[SMEM, VMEM, VMEM],
        out_specs=[VMEM] * chips,
        compiler_params=pltpu.CompilerParams(vmem_limit_bytes=16 * 1024 * 1024),
        cost_estimate=pl.CostEstimate(flops=1_000_000, bytes_accessed=1_200_000, transcendentals=0),
        name="arrange_chips",
    )(place, mine, got)


def join_kernel(count, place_ref, *refs):
    chunk_refs, out_ref, scratch_ref = refs[:-2], refs[-2], refs[-1]
    chip, core = place_ref[0] // 2, place_ref[0] % 2
    lines = chunk_refs[0].shape[0] - 16
    totals = totals_of([ref[lines:, :] for ref in chunk_refs])
    inverse = [1.0 / (total / count + 1e-06) for total in totals]
    run = lines // 2 // HYPS
    for offset, ref in zip(chip_order(len(chunk_refs)), chunk_refs):
        for part in range(2):
            start = pl.multiple_of(((chip ^ offset) * 2 + (core ^ part)) * run, run)
            for hyp in range(HYPS):
                first = (part * HYPS + hyp) * run
                scratch_ref[hyp, pl.ds(start, run), :] = ref[first : first + run, :].astype(F32) * inverse[hyp]
    beams = out_ref.shape[1]
    step = scratch_ref.shape[1] // beams
    for hyp in range(HYPS):
        for line in range(step):
            half, block = divmod(line, step // 2)
            lane = block * PAIR + half * BLOCK
            out_ref[hyp, :, lane : lane + BLOCK] = scratch_ref[hyp, pl.ds(line, beams, stride=step), :].astype(BF16)


def join(place, chunks, count, beams):
    lines = chunks[0].shape[0] - 16
    rows = lines // HYPS * len(chunks)
    return pl.pallas_call(
        functools.partial(join_kernel, count),
        out_shape=jax.ShapeDtypeStruct((HYPS, beams, rows // beams * BLOCK), BF16),
        in_specs=[SMEM] + [VMEM] * len(chunks),
        out_specs=VMEM,
        scratch_shapes=[pltpu.VMEM((HYPS, rows, BLOCK), F32)],
        compiler_params=pltpu.CompilerParams(vmem_limit_bytes=16 * 1024 * 1024),
        cost_estimate=pl.CostEstimate(flops=1_000_000, bytes_accessed=1_200_000, transcendentals=0),
        name="scale_power",
    )(place, *chunks)


def exchange(value, offset, segments):
    return lax.ppermute(value, "tm", [(index, index ^ offset) for index in range(segments)])


def body(signal, warp_blocks, taps, tap_weights, replica):
    segments = lax.axis_size("tm")
    beams = signal.shape[0] // segments
    samples = signal.shape[1] * segments
    count = float(BEAMS * samples)
    paired = segments == 16
    place = lax.axis_index("tm").astype(jnp.int32).reshape(1)
    received = lax.all_to_all(spread(signal, segments), "tm", split_axis=0, concat_axis=0, tiled=True)
    tables = transform_tables(samples // PAIR)
    interp, chosen, spectrum = prepare(replica, taps, tap_weights, warp_blocks, tables)
    sent = correlate(
        place, received.reshape(-1, BLOCK), interp, chosen, spectrum, tables, beams, segments, paired
    )
    if not paired:
        back = lax.all_to_all(sent, "tm", split_axis=0, concat_axis=0, tiled=True)
        return finish(back, count, beams)
    mine, theirs = sent
    chips = segments // 2
    chunks = arrange(place, mine, exchange(theirs, 1, segments), chips)
    arrived = [
        exchange(chunk, 2 * offset, segments) if offset else chunk for offset, chunk in zip(chip_order(chips), chunks)
    ]
    return join(place, arrived, count, signal.shape[0])


def solution(mesh):
    in_specs = (
        P("groups", "tm"),
        P("groups", None),
        P("groups", None, None),
        P("groups", None, None),
        P(),
    )
    out_specs = P("groups", None, "tm")
    return jax.shard_map(body, mesh=mesh, in_specs=in_specs, out_specs=out_specs, check_vma=False)
```

```python
import functools
import math

import jax
import jax.numpy as jnp
import numpy as np
from jax import lax
from jax.experimental import pallas as pl
from jax.experimental.pallas import tpu as pltpu
from jax.sharding import PartitionSpec as P

BEAMS = 64
BLOCK = 128
PAIR = 2 * BLOCK
TAPS = 8
REPLICA = 16384
HYPS = 2
F32 = jnp.float32
BF16 = jnp.bfloat16
VMEM = pl.BlockSpec(memory_space=pltpu.VMEM)
SMEM = pl.BlockSpec(memory_space=pltpu.SMEM)
ANY = pl.BlockSpec(memory_space=pl.ANY)


def transform_tables(points, segments):
    k, p = np.arange(points)[:, None], np.arange(points)[None, :]
    angle = 2.0 * math.pi * (k * p % points) / points
    cos, sin = np.cos(angle), np.sin(angle)
    left = np.block([[cos, sin], [-sin, cos]]).astype(np.float32)
    k, p = np.arange(PAIR)[:, None], np.arange(PAIR)[None, :]
    angle = 2.0 * math.pi * (k * p % PAIR) / PAIR
    cos, sin = np.cos(angle), np.sin(angle)
    right = np.block([[cos, -sin], [sin, cos]]).astype(np.float32)
    k, q = np.arange(points)[:, None], np.arange(PAIR)[None, :]
    angle = 2.0 * math.pi * (k * q) / (points * PAIR)
    turn = np.concatenate([np.cos(angle), -np.sin(angle)], axis=1).astype(np.float32)
    parts = []
    for table in (left, right):
        high = table.astype(jnp.bfloat16)
        low = (table - high.astype(np.float32)).astype(jnp.bfloat16)
        parts.append(np.concatenate([high, low], axis=0))
    halves = parts[0].reshape(4, segments // 2, 2, points // segments, 2 * points).transpose(2, 0, 1, 3, 4)
    halves = halves.reshape(2, 2 * points, 2 * points)
    return jnp.asarray(parts[0]), jnp.asarray(parts[1]), jnp.asarray(turn), jnp.asarray(halves)


def split(value):
    high = value.astype(BF16)
    return high, (value - high.astype(F32)).astype(BF16)


def dot(left, right):
    return jnp.dot(left, right, preferred_element_type=F32)


def spread_kernel(signal_ref, out_ref):
    upper = lax.broadcasted_iota(jnp.int32, (8, BLOCK), 0) < 4
    groups, blocks = signal_ref.shape[0] // 16, signal_ref.shape[1] // BLOCK
    for group in range(groups):
        for quad in range(0, blocks, 4):
            tiles = []
            for block in range(quad, quad + 4):
                value = signal_ref[group * 16 : group * 16 + 16, block * BLOCK : (block + 1) * BLOCK].astype(F32)
                tiles.append((value[:8], value[8:]))
            for half in range(2):
                parts = [tile[half] for tile in tiles]
                turned = [pltpu.roll(part, 4, 0) for part in parts]
                first = [jnp.where(upper, parts[d], turned[d + 1]) for d in (0, 2)]
                second = [jnp.where(upper, turned[d], parts[d + 1]) for d in (0, 2)]
                device = group * 4 + half * 2
                rows = slice(quad * 4, quad * 4 + 16)
                out_ref[device, rows, :] = jnp.concatenate(first, axis=0).astype(BF16)
                out_ref[device + 1, rows, :] = jnp.concatenate(second, axis=0).astype(BF16)


def spread(signal, segments):
    beams, blocks = signal.shape[0] // segments, signal.shape[1] // BLOCK
    if beams != 4 or signal.shape[0] % 16 or blocks % 4:
        send = signal.reshape(segments, beams, blocks, BLOCK).transpose(0, 2, 1, 3)
        return send.reshape(segments, blocks * beams, BLOCK)
    return pl.pallas_call(
        spread_kernel,
        out_shape=jax.ShapeDtypeStruct((segments, blocks * beams, BLOCK), BF16),
        in_specs=[VMEM],
        out_specs=VMEM,
        name="spread_beams",
    )(signal)


def prepare_kernel(replica_ref, taps_ref, weights_ref, sources_ref, left_ref, right_ref, turn_ref, interp_ref, chosen_ref, spectrum_ref):
    window = lax.broadcasted_iota(jnp.int32, (PAIR, BLOCK), 0)
    for hyp in range(HYPS):
        total = jnp.zeros((PAIR, BLOCK), F32)
        for tap in range(TAPS):
            hit = taps_ref[hyp, tap : tap + 1, :] == window
            total = total + jnp.where(hit, weights_ref[hyp, tap : tap + 1, :], 0.0)
        interp_ref[:, hyp * BLOCK : (hyp + 1) * BLOCK] = total.astype(BF16)

    blocks = chosen_ref.shape[1]
    column = lax.broadcasted_iota(jnp.int32, (blocks, blocks), 1)
    for hyp in range(HYPS):
        rows = slice(hyp * blocks, (hyp + 1) * blocks)
        chosen_ref[rows, :] = (sources_ref[rows, :] == column).astype(F32).astype(BF16)

    points = turn_ref.shape[0]
    lines = replica_ref.shape[0]
    high, low = split(replica_ref[...])
    both = dot(left_ref[:, :lines], high)
    value = both[: 2 * points] + both[2 * points :] + dot(left_ref[: 2 * points, :lines], low)
    value_re, value_im = value[:points], value[points:]
    turn_re, turn_im = turn_ref[:, :PAIR], turn_ref[:, PAIR:]
    turned = jnp.concatenate(
        [value_re * turn_re - value_im * turn_im, value_re * turn_im + value_im * turn_re], axis=1
    )
    high, low = split(turned)
    upper, lower = right_ref[: 2 * PAIR, :], right_ref[2 * PAIR :, :]
    value = (dot(high, upper) + dot(high, lower) + dot(low, upper)) * (1.0 / (points * PAIR))
    spectrum_ref[:, :PAIR] = value[:, :PAIR]
    spectrum_ref[:, PAIR:] = -value[:, PAIR:]


def prepare(replica, taps, tap_weights, warp_blocks, tables):
    blocks = warp_blocks.shape[1]
    points = blocks // 2
    ordered = warp_blocks.reshape(HYPS, points, 2).transpose(0, 2, 1).reshape(HYPS * blocks, 1)
    operands = (replica.reshape(-1, PAIR), taps.transpose(0, 2, 1), tap_weights.transpose(0, 2, 1), ordered, *tables[:3])
    shapes = ((PAIR, HYPS * BLOCK), BF16), ((HYPS * blocks, blocks), BF16), ((points, 2 * PAIR), F32)

    def whole(shape):
        return pl.BlockSpec(shape, lambda g: (0,) * len(shape))

    return pl.pallas_call(
        prepare_kernel,
        grid=(1,),
        out_shape=[jax.ShapeDtypeStruct(*shape) for shape in shapes],
        in_specs=[whole(operand.shape) for operand in operands],
        out_specs=[VMEM] * len(shapes),
        compiler_params=pltpu.CompilerParams(vmem_limit_bytes=24 * 1024 * 1024),
        cost_estimate=pl.CostEstimate(flops=500_000_000, bytes_accessed=16_000_000, transcendentals=0),
        name="prepare_tables",
    )(*operands)


def split_sum(total):
    high = total.astype(BF16).astype(F32)
    middle = (total - high).astype(BF16).astype(F32)
    return high, middle, total - high - middle


def tail_of(totals):
    place = lax.broadcasted_iota(jnp.int32, (16, BLOCK), 0)
    tail = jnp.zeros((16, BLOCK), F32)
    for hyp, total in enumerate(totals):
        for index, piece in enumerate(split_sum(total)):
            tail = jnp.where(place == hyp * 3 + index, piece, tail)
    return tail.astype(BF16)


def totals_of(tails):
    place = lax.broadcasted_iota(jnp.int32, (16, BLOCK), 0)
    total = functools.reduce(jnp.add, [tail.astype(F32) for tail in tails])
    return [
        jnp.sum(jnp.where((place >= 3 * hyp) & (place < 3 * hyp + 3), total, 0.0), axis=0, keepdims=True)
        for hyp in range(HYPS)
    ]


def complex_rows(beams):
    if beams % 2:
        return [(hyp, beam, None) for hyp in range(HYPS) for beam in range(beams)]
    return [(hyp, beam, beam + 1) for hyp in range(HYPS) for beam in range(0, beams, 2)]


def transform(
    beams, source_ref, interp_ref, chosen_ref, left_ref, turn_ref, right_ref, spectrum_ref, column_ref, next_ref, block_ref, row_ref, wide_ref
):
    points = turn_ref.shape[0]
    blocks = 2 * points
    lines = source_ref.shape[0]
    rows = complex_rows(beams)
    chunk = min(512, lines)

    for start in range(0, lines, chunk):
        next_ref[start : start + chunk, :] = dot(source_ref[start : start + chunk, :], interp_ref[BLOCK:, :])
    next_ref[lines : lines + 8, :] = next_ref[0:8, :]
    for start in range(0, lines, chunk):
        value = (
            dot(source_ref[start : start + chunk, :], interp_ref[:BLOCK, :])
            + next_ref[start + beams : start + beams + chunk, :]
        )
        for hyp in range(HYPS):
            block_ref[hyp, start : start + chunk, :] = value[:, hyp * BLOCK : (hyp + 1) * BLOCK]

    for hyp in range(HYPS):
        warped = jnp.concatenate(
            [block_ref[hyp, pl.ds(beam, blocks, stride=beams), :].astype(BF16) for beam in range(beams)], axis=1
        )
        gathered = dot(chosen_ref[hyp * blocks : (hyp + 1) * blocks, :], warped).astype(BF16)
        for index, (row_hyp, *pair) in enumerate(rows):
            if row_hyp != hyp:
                continue
            for part, beam in enumerate(pair):
                for half in range(2):
                    lane = index * PAIR + half * BLOCK
                    target = (slice(part * points, (part + 1) * points), slice(lane, lane + BLOCK))
                    if beam is None:
                        column_ref[target] = jnp.zeros((points, BLOCK), BF16)
                    else:
                        column_ref[target] = gathered[
                            half * points : (half + 1) * points, beam * BLOCK : (beam + 1) * BLOCK
                        ]

    def right_product():
        value = row_ref[...]
        wide_ref[...] = dot(value, right_ref[: 2 * PAIR, :]) + dot(value, right_ref[2 * PAIR :, :])

    turn_re, turn_im = turn_ref[:, :PAIR], turn_ref[:, PAIR:]
    for index in range(len(rows)):
        real, imag = left_product(left_ref[...], column_ref, index)
        place = slice(index * points, (index + 1) * points)
        row_ref[place, :PAIR] = (real * turn_re - imag * turn_im).astype(BF16)
        row_ref[place, PAIR:] = (real * turn_im + imag * turn_re).astype(BF16)
    right_product()
    spectrum_re, spectrum_im = spectrum_ref[:, :PAIR], spectrum_ref[:, PAIR:]
    sums = [jnp.zeros((8, PAIR), F32) for _ in range(HYPS)]
    for index, (hyp, _, _) in enumerate(rows):
        place = slice(index * points, (index + 1) * points)
        real, imag = wide_ref[place, :PAIR], wide_ref[place, PAIR:]
        new_re = real * spectrum_re - imag * spectrum_im
        new_im = real * spectrum_im + imag * spectrum_re
        square = new_re * new_re + new_im * new_im
        sums[hyp] = sums[hyp] + jnp.sum(square.reshape(points // 8, 8, PAIR), axis=0)
        row_ref[place, PAIR:] = new_re.astype(BF16)
        row_ref[place, :PAIR] = new_im.astype(BF16)
    right_product()
    for index in range(len(rows)):
        place = slice(index * points, (index + 1) * points)
        lanes = slice(index * PAIR, (index + 1) * PAIR)
        imag, real = wide_ref[place, :PAIR], wide_ref[place, PAIR:]
        column_ref[points:, lanes] = (real * turn_re + imag * turn_im).astype(BF16)
        column_ref[:points, lanes] = (imag * turn_re - real * turn_im).astype(BF16)
    return [
        jnp.sum(jnp.sum(value, axis=1, keepdims=True), axis=0, keepdims=True) * (points * PAIR) for value in sums
    ]


def left_product(matrix, column_ref, index):
    both = dot(matrix, column_ref[:, index * PAIR : (index + 1) * PAIR])
    value = both[: both.shape[0] // 2] + both[both.shape[0] // 2 :]
    return value[: value.shape[0] // 2], value[value.shape[0] // 2 :]


def powers(matrix, column_ref, beams):
    for index, (hyp, real_beam, imag_beam) in enumerate(complex_rows(beams)):
        imag, real = left_product(matrix, column_ref, index)
        for beam, value in ((real_beam, real), (imag_beam, imag)):
            if beam is not None:
                yield hyp * beams + beam, value * value


def store_powers(matrix, column_ref, beams, segments, target):
    for number, power in powers(matrix, column_ref, beams):
        share = power.shape[0] // segments
        for segment in range(segments):
            piece = power[segment * share : (segment + 1) * share, :]
            piece = jnp.concatenate([piece[:, :BLOCK], piece[:, BLOCK:]], axis=0)
            target(segment)[number * 2 * share : (number + 1) * 2 * share, :] = piece.astype(BF16)


def correlate_kernel(beams, segments, source_ref, *refs):
    tables, out_ref, scratch = refs[:6], refs[6], refs[7:]
    totals = transform(beams, source_ref, *tables, *scratch)
    store_powers(tables[2][...], scratch[0], beams, segments, lambda segment: out_ref.at[segment])
    tail = tail_of(totals)
    for segment in range(segments):
        out_ref[segment, out_ref.shape[1] - 16 :, :] = tail


def first_half_kernel(beams, segments, place_ref, source_ref, *refs):
    tables, halves_ref, column_ref, theirs_ref, scratch = refs[:6], refs[6], refs[7], refs[8], refs[9:]
    totals = transform(beams, source_ref, *tables, column_ref, *scratch)
    chips = segments // 2
    lines = (theirs_ref.shape[0] - 16) // chips
    parity = (place_ref[0] + 1) % 2
    store_powers(
        halves_ref[parity], column_ref, beams, chips, lambda chip: theirs_ref.at[chip * lines : (chip + 1) * lines]
    )
    theirs_ref[chips * lines :, :] = tail_of(totals)


def second_half_kernel(beams, segments, place_ref, column_ref, halves_ref, mine_ref):
    chips = segments // 2
    lines = mine_ref.shape[0] // chips
    parity = place_ref[0] % 2
    store_powers(
        halves_ref[parity], column_ref, beams, chips, lambda chip: mine_ref.at[chip * lines : (chip + 1) * lines]
    )


def correlate_shapes(lines, points, beams):
    count = len(complex_rows(beams))
    column = ((2 * points, count * PAIR), BF16)
    scratch = [
        ((lines + 8, PAIR), F32),
        ((HYPS, lines, BLOCK), F32),
        ((count * points, 2 * PAIR), BF16),
        ((count * points, 2 * PAIR), F32),
    ]
    return column, scratch


def correlate(source, interp, chosen, spectrum, tables, beams, segments):
    left, right, turn, _ = tables
    points = turn.shape[0]
    column, scratch = correlate_shapes(source.shape[0], points, beams)
    return pl.pallas_call(
        functools.partial(correlate_kernel, beams, segments),
        out_shape=jax.ShapeDtypeStruct((segments, HYPS * beams * 2 * (points // segments) + 16, BLOCK), BF16),
        in_specs=[VMEM] * 7,
        out_specs=VMEM,
        scratch_shapes=[pltpu.VMEM(*shape) for shape in (column, *scratch)],
        compiler_params=pltpu.CompilerParams(vmem_limit_bytes=48 * 1024 * 1024),
        cost_estimate=pl.CostEstimate(flops=4_000_000_000, bytes_accessed=6_000_000, transcendentals=0),
        name="warp_correlate",
    )(source, interp, chosen, left, turn, right, spectrum)


def correlate_in_halves(place, source, interp, chosen, spectrum, tables, beams, segments):
    left, right, turn, halves = tables
    points = turn.shape[0]
    column, scratch = correlate_shapes(source.shape[0], points, beams)
    rows = segments // 2 * HYPS * beams * 2 * (points // segments)
    columns, theirs = pl.pallas_call(
        functools.partial(first_half_kernel, beams, segments),
        out_shape=(jax.ShapeDtypeStruct(*column), jax.ShapeDtypeStruct((rows + 16, BLOCK), BF16)),
        in_specs=[SMEM] + [VMEM] * 8,
        out_specs=(VMEM, VMEM),
        scratch_shapes=[pltpu.VMEM(*shape) for shape in scratch],
        compiler_params=pltpu.CompilerParams(vmem_limit_bytes=24 * 1024 * 1024),
        cost_estimate=pl.CostEstimate(flops=4_000_000_000, bytes_accessed=6_000_000, transcendentals=0),
        name="warp_correlate",
    )(place, source, interp, chosen, left, turn, right, spectrum, halves)
    mine = pl.pallas_call(
        functools.partial(second_half_kernel, beams, segments),
        out_shape=jax.ShapeDtypeStruct((rows, BLOCK), BF16),
        in_specs=[SMEM, VMEM, VMEM],
        out_specs=VMEM,
        compiler_params=pltpu.CompilerParams(vmem_limit_bytes=16 * 1024 * 1024),
        cost_estimate=pl.CostEstimate(flops=1_000_000_000, bytes_accessed=2_000_000, transcendentals=0),
        name="second_half",
    )(place, columns, halves)
    return theirs, mine


def finish_kernel(count, power_ref, sums_ref, out_ref, scratch_ref):
    hyp = pl.program_id(0)
    sums = sums_ref[...].astype(F32)
    place = lax.broadcasted_iota(jnp.int32, sums.shape, 1)
    picked = jnp.where((place >= 3 * hyp) & (place < 3 * hyp + 3), sums, 0.0)
    total = jnp.sum(jnp.sum(picked, axis=0), axis=0, keepdims=True)
    inverse = 1.0 / (total / count + 1e-06)
    devices, lines, _ = power_ref.shape
    for device in range(devices):
        scratch_ref[device * lines : (device + 1) * lines, :] = power_ref[device].astype(F32) * inverse
    beams = out_ref.shape[1]
    step = devices * lines // beams
    for line in range(step):
        half, block = divmod(line, step // 2)
        lane = block * PAIR + half * BLOCK
        out_ref[0, :, lane : lane + BLOCK] = scratch_ref[pl.ds(line, beams, stride=step), :].astype(BF16)


def finish(received, count, beams):
    segments, out_rows, _ = received.shape
    lines = (out_rows - 16) // HYPS
    samples = lines // beams * BLOCK
    return pl.pallas_call(
        functools.partial(finish_kernel, count),
        grid=(HYPS,),
        out_shape=jax.ShapeDtypeStruct((HYPS, segments * beams, samples), BF16),
        in_specs=[
            pl.BlockSpec((segments, lines, BLOCK), lambda g: (0, g, 0)),
            pl.BlockSpec((segments, 16, BLOCK), lambda g: (0, HYPS * lines // 16, 0)),
        ],
        out_specs=pl.BlockSpec((1, segments * beams, samples), lambda g: (g, 0, 0)),
        scratch_shapes=[pltpu.VMEM((segments * lines, BLOCK), F32)],
        cost_estimate=pl.CostEstimate(flops=1_000_000, bytes_accessed=1_200_000, transcendentals=0),
        name="scale_power",
    )(received, received)


def chip_order(chips):
    far, near = range(chips // 2, chips), [*range(1, chips // 2), 0]
    return [offset for pair in zip(far, near) for offset in pair][:-1] + [0]


def arrange_kernel(place_ref, mine_ref, sums_ref, got_ref, *out_refs):
    chip = place_ref[0] // 2
    count = len(out_refs)
    lines = mine_ref.shape[0] // count
    tails = [ref[count * lines :, :] for ref in (sums_ref, got_ref)]
    tail = tail_of([total[:, :1] for total in totals_of(tails)])
    for offset, out_ref in zip(chip_order(count), out_refs):
        rows = pl.ds(pl.multiple_of((chip ^ offset) * lines, lines), lines)
        out_ref[:lines, :] = mine_ref[rows, :]
        out_ref[lines : 2 * lines, :] = got_ref[rows, :]
        out_ref[2 * lines :, :] = tail


def arrange(place, mine, theirs, got, chips):
    lines = mine.shape[0] // chips
    shape = jax.ShapeDtypeStruct((2 * lines + 16, BLOCK), BF16)
    return pl.pallas_call(
        arrange_kernel,
        out_shape=[shape] * chips,
        in_specs=[SMEM] + [VMEM] * 3,
        out_specs=[VMEM] * chips,
        compiler_params=pltpu.CompilerParams(vmem_limit_bytes=16 * 1024 * 1024),
        cost_estimate=pl.CostEstimate(flops=1_000_000, bytes_accessed=1_200_000, transcendentals=0),
        name="arrange_chips",
    )(place, mine, theirs, got)


def join_kernel(count, place_ref, *refs):
    chunk_refs, out_ref, scratch_ref = refs[:-2], refs[-2], refs[-1]
    chip, core = place_ref[0] // 2, place_ref[0] % 2
    lines = chunk_refs[0].shape[0] - 16
    totals = totals_of([ref[lines:, :] for ref in chunk_refs])
    inverse = [1.0 / (total / count + 1e-06) for total in totals]
    run = lines // 2 // HYPS
    for offset, ref in zip(chip_order(len(chunk_refs)), chunk_refs):
        for part in range(2):
            start = pl.multiple_of(((chip ^ offset) * 2 + (core ^ part)) * run, run)
            for hyp in range(HYPS):
                first = (part * HYPS + hyp) * run
                scratch_ref[hyp, pl.ds(start, run), :] = ref[first : first + run, :].astype(F32) * inverse[hyp]
    beams = out_ref.shape[1]
    step = scratch_ref.shape[1] // beams
    for hyp in range(HYPS):
        for line in range(step):
            half, block = divmod(line, step // 2)
            lane = block * PAIR + half * BLOCK
            out_ref[hyp, :, lane : lane + BLOCK] = scratch_ref[hyp, pl.ds(line, beams, stride=step), :].astype(BF16)


def join(place, chunks, count, beams):
    lines = chunks[0].shape[0] - 16
    rows = lines // HYPS * len(chunks)
    return pl.pallas_call(
        functools.partial(join_kernel, count),
        out_shape=jax.ShapeDtypeStruct((HYPS, beams, rows // beams * BLOCK), BF16),
        in_specs=[SMEM] + [VMEM] * len(chunks),
        out_specs=VMEM,
        scratch_shapes=[pltpu.VMEM((HYPS, rows, BLOCK), F32)],
        compiler_params=pltpu.CompilerParams(vmem_limit_bytes=16 * 1024 * 1024),
        cost_estimate=pl.CostEstimate(flops=1_000_000, bytes_accessed=1_200_000, transcendentals=0),
        name="scale_power",
    )(place, *chunks)


def exchange(value, offset, segments):
    return lax.ppermute(value, "tm", [(index, index ^ offset) for index in range(segments)])


def body(signal, warp_blocks, taps, tap_weights, replica):
    segments = lax.axis_size("tm")
    beams = signal.shape[0] // segments
    samples = signal.shape[1] * segments
    count = float(BEAMS * samples)
    received = lax.all_to_all(spread(signal, segments), "tm", split_axis=0, concat_axis=0, tiled=True)
    source = received.reshape(-1, BLOCK)
    tables = transform_tables(samples // PAIR, segments)
    interp, chosen, spectrum = prepare(replica, taps, tap_weights, warp_blocks, tables)
    if segments != 16:
        sent = correlate(source, interp, chosen, spectrum, tables, beams, segments)
        back = lax.all_to_all(sent, "tm", split_axis=0, concat_axis=0, tiled=True)
        return finish(back, count, beams)
    place = lax.axis_index("tm").astype(jnp.int32).reshape(1)
    theirs, mine = correlate_in_halves(place, source, interp, chosen, spectrum, tables, beams, segments)
    chips = segments // 2
    chunks = arrange(place, mine, theirs, exchange(theirs, 1, segments), chips)
    arrived = [
        exchange(chunk, 2 * offset, segments) if offset else chunk for offset, chunk in zip(chip_order(chips), chunks)
    ]
    return join(place, arrived, count, signal.shape[0])


def solution(mesh):
    in_specs = (
        P("groups", "tm"),
        P("groups", None),
        P("groups", None, None),
        P("groups", None, None),
        P(),
    )
    out_specs = P("groups", None, "tm")
    return jax.shard_map(body, mesh=mesh, in_specs=in_specs, out_specs=out_specs, check_vma=False)
```

```python
import functools
import math

import jax
import jax.numpy as jnp
import numpy as np
from jax import lax
from jax.experimental import pallas as pl
from jax.experimental.pallas import tpu as pltpu
from jax.sharding import PartitionSpec as P

BEAMS = 64
BLOCK = 128
PAIR = 2 * BLOCK
TAPS = 8
REPLICA = 16384
HYPS = 2
F32 = jnp.float32
BF16 = jnp.bfloat16
VMEM = pl.BlockSpec(memory_space=pltpu.VMEM)
SMEM = pl.BlockSpec(memory_space=pltpu.SMEM)
ANY = pl.BlockSpec(memory_space=pl.ANY)


def transform_tables(points, segments):
    k, p = np.arange(points)[:, None], np.arange(points)[None, :]
    angle = 2.0 * math.pi * (k * p % points) / points
    cos, sin = np.cos(angle), np.sin(angle)
    left = np.block([[cos, sin], [-sin, cos]]).astype(np.float32)
    k, p = np.arange(PAIR)[:, None], np.arange(PAIR)[None, :]
    angle = 2.0 * math.pi * (k * p % PAIR) / PAIR
    cos, sin = np.cos(angle), np.sin(angle)
    right = np.block([[cos, -sin], [sin, cos]]).astype(np.float32)
    k, q = np.arange(points)[:, None], np.arange(PAIR)[None, :]
    angle = 2.0 * math.pi * (k * q) / (points * PAIR)
    turn = np.concatenate([np.cos(angle), -np.sin(angle)], axis=1).astype(np.float32)
    parts = []
    for table in (left, right):
        high = table.astype(jnp.bfloat16)
        low = (table - high.astype(np.float32)).astype(jnp.bfloat16)
        parts.append(np.concatenate([high, low], axis=0))
    halves = parts[0].reshape(4, segments // 2, 2, points // segments, 2 * points).transpose(2, 0, 1, 3, 4)
    halves = halves.reshape(2, 2 * points, 2 * points)
    return jnp.asarray(parts[0]), jnp.asarray(parts[1]), jnp.asarray(turn), jnp.asarray(halves)


def split(value):
    high = value.astype(BF16)
    return high, (value - high.astype(F32)).astype(BF16)


def dot(left, right):
    return jnp.dot(left, right, preferred_element_type=F32)


def spread(signal, segments):
    beams, blocks = signal.shape[0] // segments, signal.shape[1] // BLOCK
    send = signal.reshape(segments, beams, blocks, BLOCK).transpose(0, 2, 1, 3)
    return send.reshape(segments, blocks * beams, BLOCK)


def prepare_kernel(
    segments, paired, place_ref, replica_ref, taps_ref, weights_ref, sources_ref, left_ref, right_ref, turn_ref, interp_ref, chosen_ref, spectrum_ref
):
    core = place_ref[0] % 2
    blocks = chosen_ref.shape[1]
    points = blocks // 2
    window = lax.broadcasted_iota(jnp.int32, (PAIR, BLOCK), 0)
    row = lax.broadcasted_iota(jnp.int32, (blocks, blocks), 0)
    column = lax.broadcasted_iota(jnp.int32, (blocks, blocks), 1)
    order = (column == row % points * 2 + row // points).astype(F32).astype(BF16)
    held = row
    if paired:
        chips, local = segments // 2, blocks // segments
        held = row % chips * 2 * local + (row // points + core) % 2 * local + row // chips % local
    for index, hyp in enumerate([core] if paired else range(HYPS)):
        taps, weights = taps_ref[hyp], weights_ref[hyp]
        total = jnp.zeros((PAIR, BLOCK), F32)
        for tap in range(TAPS):
            total = total + jnp.where(taps[tap : tap + 1, :] == window, weights[tap : tap + 1, :], 0.0)
        if paired:
            interp_ref[...] = jnp.concatenate([total[:BLOCK], total[BLOCK:]], axis=1).astype(BF16)
        else:
            interp_ref[:, hyp * BLOCK : (hyp + 1) * BLOCK] = total.astype(BF16)
        hits = (held == sources_ref[pl.ds(hyp, 1), :]).astype(F32).astype(BF16)
        picked = lax.dot_general(order, hits, (((1,), (1,)), ((), ())), preferred_element_type=F32)
        chosen_ref[index * blocks : (index + 1) * blocks, :] = picked.astype(BF16)

    lines = replica_ref.shape[0] // 2
    high, low = split(jnp.concatenate([replica_ref[pl.ds(half, lines, stride=2), :] for half in range(2)], axis=1))
    both = dot(left_ref[:, :lines], high)
    value = both[: 2 * points] + both[2 * points :] + dot(left_ref[: 2 * points, :lines], low)
    value_re, value_im = value[:points], value[points:]
    turn_re, turn_im = turn_ref[:, :PAIR], turn_ref[:, PAIR:]
    turned = jnp.concatenate(
        [value_re * turn_re - value_im * turn_im, value_re * turn_im + value_im * turn_re], axis=1
    )
    high, low = split(turned)
    upper, lower = right_ref[: 2 * PAIR, :], right_ref[2 * PAIR :, :]
    value = (dot(high, upper) + dot(high, lower) + dot(low, upper)) * (1.0 / (points * PAIR))
    spectrum_ref[:, :PAIR] = value[:, :PAIR]
    spectrum_ref[:, PAIR:] = -value[:, PAIR:]


def prepare(place, replica, taps, tap_weights, warp_blocks, tables, segments, paired):
    blocks = warp_blocks.shape[1]
    points = blocks // 2
    taps, tap_weights = taps.transpose(0, 2, 1), tap_weights.transpose(0, 2, 1)
    operands = (replica.reshape(-1, BLOCK), taps, tap_weights, warp_blocks, *tables[:3])
    interp, count = ((BLOCK, PAIR), 1) if paired else ((PAIR, HYPS * BLOCK), HYPS)
    shapes = (interp, BF16), ((count * blocks, blocks), BF16), ((points, 2 * PAIR), F32)

    def whole(shape):
        return pl.BlockSpec(shape, lambda g: (0,) * len(shape))

    return pl.pallas_call(
        functools.partial(prepare_kernel, segments, paired),
        grid=(1,),
        out_shape=[jax.ShapeDtypeStruct(*shape) for shape in shapes],
        in_specs=[SMEM] + [whole(operand.shape) for operand in operands],
        out_specs=[VMEM] * len(shapes),
        compiler_params=pltpu.CompilerParams(vmem_limit_bytes=24 * 1024 * 1024),
        cost_estimate=pl.CostEstimate(flops=500_000_000, bytes_accessed=16_000_000, transcendentals=0),
        name="prepare_tables",
    )(place, *operands)


def split_sum(total):
    high = total.astype(BF16).astype(F32)
    middle = (total - high).astype(BF16).astype(F32)
    return high, middle, total - high - middle


def tail_of(totals):
    place = lax.broadcasted_iota(jnp.int32, (16, BLOCK), 0)
    tail = jnp.zeros((16, BLOCK), F32)
    for hyp, total in enumerate(totals):
        for index, piece in enumerate(split_sum(total)):
            tail = jnp.where(place == hyp * 3 + index, piece, tail)
    return tail.astype(BF16)


def totals_of(tails):
    place = lax.broadcasted_iota(jnp.int32, (16, BLOCK), 0)
    total = functools.reduce(jnp.add, [tail.astype(F32) for tail in tails])
    return [
        jnp.sum(jnp.where((place >= 3 * hyp) & (place < 3 * hyp + 3), total, 0.0), axis=0, keepdims=True)
        for hyp in range(HYPS)
    ]


def complex_rows(hyps, beams):
    if beams % 2:
        return [(hyp, beam, None) for hyp in range(hyps) for beam in range(beams)]
    return [(hyp, beam, beam + 1) for hyp in range(hyps) for beam in range(0, beams, 2)]


def warp(beams, source_ref, interp_ref, chosen_ref, column_ref, next_ref, block_ref):
    lines = source_ref.shape[0]
    blocks = lines // beams
    chunk = min(512, lines)

    for start in range(0, lines, chunk):
        next_ref[start : start + chunk, :] = dot(source_ref[start : start + chunk, :], interp_ref[BLOCK:, :])
    next_ref[lines : lines + 8, :] = next_ref[0:8, :]
    for start in range(0, lines, chunk):
        value = (
            dot(source_ref[start : start + chunk, :], interp_ref[:BLOCK, :])
            + next_ref[start + beams : start + beams + chunk, :]
        )
        for hyp in range(HYPS):
            block_ref[hyp, start : start + chunk, :] = value[:, hyp * BLOCK : (hyp + 1) * BLOCK]
    for hyp in range(HYPS):
        warped = jnp.concatenate(
            [block_ref[hyp, pl.ds(beam, blocks, stride=beams), :].astype(BF16) for beam in range(beams)], axis=1
        )
        choose(hyp, HYPS, beams, chosen_ref[hyp * blocks : (hyp + 1) * blocks, :], warped, column_ref)


def choose(hyp, hyps, beams, chosen, warped, column_ref):
    gathered = dot(chosen, warped).astype(BF16)
    points = gathered.shape[0] // 2
    for index, (row_hyp, *pair) in enumerate(complex_rows(hyps, beams)):
        if row_hyp != hyp:
            continue
        for part, beam in enumerate(pair):
            for half in range(2):
                lane = index * PAIR + half * BLOCK
                target = (slice(part * points, (part + 1) * points), slice(lane, lane + BLOCK))
                if beam is None:
                    column_ref[target] = jnp.zeros((points, BLOCK), BF16)
                else:
                    column_ref[target] = gathered[
                        half * points : (half + 1) * points, beam * BLOCK : (beam + 1) * BLOCK
                    ]


def warp_paired(beams, core, own_ref, other_ref, interp_ref, chosen_ref, column_ref, next_ref, block_ref):
    lines, samples = own_ref.shape
    local = samples // BLOCK
    for part, source_ref in enumerate((own_ref, other_ref)):
        stacked = jnp.concatenate(
            [source_ref[:, block * BLOCK : (block + 1) * BLOCK] for block in range(local)], axis=0
        )
        value = dot(stacked, interp_ref[...])
        block_ref[part] = value[:, :BLOCK]
        next_ref[part] = value[:, BLOCK:]
    last = (local - 1) * lines
    for part in range(2):
        block_ref[part, :last, :] = block_ref[part, :last, :] + next_ref[part, lines:, :]
        after = next_ref[1 - part, :lines, :]
        turned = jnp.concatenate([after[beams:], after[:beams]], axis=0)
        block_ref[part, last:, :] = block_ref[part, last:, :] + jnp.where((core + part) % 2 == 0, after, turned)
    count = local * lines // beams
    warped = [
        jnp.concatenate(
            [block_ref[part, pl.ds(beam, count, stride=beams), :].astype(BF16) for beam in range(beams)], axis=1
        )
        for part in range(2)
    ]
    choose(0, 1, beams, chosen_ref[...], jnp.concatenate(warped, axis=0), column_ref)


def transform(hyps, beams, left_ref, turn_ref, right_ref, spectrum_ref, column_ref, row_ref, wide_ref):
    points = turn_ref.shape[0]
    rows = complex_rows(hyps, beams)

    def right_product():
        value = row_ref[...]
        wide_ref[...] = dot(value, right_ref[: 2 * PAIR, :]) + dot(value, right_ref[2 * PAIR :, :])

    turn_re, turn_im = turn_ref[:, :PAIR], turn_ref[:, PAIR:]
    for index in range(len(rows)):
        real, imag = left_product(left_ref[...], column_ref, index)
        place = slice(index * points, (index + 1) * points)
        row_ref[place, :PAIR] = (real * turn_re - imag * turn_im).astype(BF16)
        row_ref[place, PAIR:] = (real * turn_im + imag * turn_re).astype(BF16)
    right_product()
    spectrum_re, spectrum_im = spectrum_ref[:, :PAIR], spectrum_ref[:, PAIR:]
    sums = [jnp.zeros((8, PAIR), F32) for _ in range(hyps)]
    for index, (hyp, _, _) in enumerate(rows):
        place = slice(index * points, (index + 1) * points)
        real, imag = wide_ref[place, :PAIR], wide_ref[place, PAIR:]
        new_re = real * spectrum_re - imag * spectrum_im
        new_im = real * spectrum_im + imag * spectrum_re
        square = new_re * new_re + new_im * new_im
        sums[hyp] = sums[hyp] + jnp.sum(square.reshape(points // 8, 8, PAIR), axis=0)
        row_ref[place, PAIR:] = new_re.astype(BF16)
        row_ref[place, :PAIR] = new_im.astype(BF16)
    right_product()
    for index in range(len(rows)):
        place = slice(index * points, (index + 1) * points)
        lanes = slice(index * PAIR, (index + 1) * PAIR)
        imag, real = wide_ref[place, :PAIR], wide_ref[place, PAIR:]
        column_ref[points:, lanes] = (real * turn_re + imag * turn_im).astype(BF16)
        column_ref[:points, lanes] = (imag * turn_re - real * turn_im).astype(BF16)
    return [
        jnp.sum(jnp.sum(value, axis=1, keepdims=True), axis=0, keepdims=True) * (points * PAIR) for value in sums
    ]


def left_product(matrix, column_ref, index):
    both = dot(matrix, column_ref[:, index * PAIR : (index + 1) * PAIR])
    value = both[: both.shape[0] // 2] + both[both.shape[0] // 2 :]
    return value[: value.shape[0] // 2], value[value.shape[0] // 2 :]


def store_powers(matrix, column_ref, hyps, beams, segments, target):
    for index, (hyp, real_beam, imag_beam) in enumerate(complex_rows(hyps, beams)):
        imag, real = left_product(matrix, column_ref, index)
        for beam, value in ((real_beam, real), (imag_beam, imag)):
            if beam is None:
                continue
            number = hyp * beams + beam
            power = value * value
            share = power.shape[0] // segments
            for segment in range(segments):
                piece = power[segment * share : (segment + 1) * share, :]
                piece = jnp.concatenate([piece[:, :BLOCK], piece[:, BLOCK:]], axis=0)
                target(segment)[number * 2 * share : (number + 1) * 2 * share, :] = piece.astype(BF16)


def correlate_kernel(beams, segments, source_ref, interp_ref, chosen_ref, left_ref, turn_ref, right_ref, spectrum_ref, *refs):
    out_ref, column_ref, row_ref, wide_ref, next_ref, block_ref = refs
    warp(beams, source_ref, interp_ref, chosen_ref, column_ref, next_ref, block_ref)
    totals = transform(HYPS, beams, left_ref, turn_ref, right_ref, spectrum_ref, column_ref, row_ref, wide_ref)
    store_powers(left_ref[...], column_ref, HYPS, beams, segments, lambda segment: out_ref.at[segment])
    tail = tail_of(totals)
    for segment in range(segments):
        out_ref[segment, out_ref.shape[1] - 16 :, :] = tail


def first_half_kernel(
    beams, segments, place_ref, own_ref, other_ref, interp_ref, chosen_ref, left_ref, turn_ref, right_ref, spectrum_ref, halves_ref, *refs
):
    column_ref, theirs_ref, row_ref, wide_ref, next_ref, block_ref = refs
    core = place_ref[0] % 2
    warp_paired(beams, core, own_ref, other_ref, interp_ref, chosen_ref, column_ref, next_ref, block_ref)
    (total,) = transform(1, beams, left_ref, turn_ref, right_ref, spectrum_ref, column_ref, row_ref, wide_ref)
    chips = segments // 2
    lines = (theirs_ref.shape[0] - 16) // chips
    store_powers(
        halves_ref[1 - core], column_ref, 1, beams, chips, lambda chip: theirs_ref.at[chip * lines : (chip + 1) * lines]
    )
    theirs_ref[chips * lines :, :] = tail_of([jnp.where(core == hyp, total, 0.0) for hyp in range(HYPS)])


def second_half_kernel(beams, segments, place_ref, column_ref, halves_ref, mine_ref):
    chips = segments // 2
    lines = mine_ref.shape[0] // chips
    store_powers(
        halves_ref[place_ref[0] % 2],
        column_ref,
        1,
        beams,
        chips,
        lambda chip: mine_ref.at[chip * lines : (chip + 1) * lines],
    )


def correlate_shapes(points, count):
    return (
        ((2 * points, count * PAIR), BF16),
        ((count * points, 2 * PAIR), BF16),
        ((count * points, 2 * PAIR), F32),
    )


def correlate(source, interp, chosen, spectrum, tables, beams, segments):
    left, right, turn, _ = tables
    points, lines = turn.shape[0], source.shape[0]
    scratch = correlate_shapes(points, len(complex_rows(HYPS, beams)))
    scratch += (((lines + 8, PAIR), F32), ((HYPS, lines, BLOCK), F32))
    return pl.pallas_call(
        functools.partial(correlate_kernel, beams, segments),
        out_shape=jax.ShapeDtypeStruct((segments, HYPS * beams * 2 * (points // segments) + 16, BLOCK), BF16),
        in_specs=[VMEM] * 7,
        out_specs=VMEM,
        scratch_shapes=[pltpu.VMEM(*shape) for shape in scratch],
        compiler_params=pltpu.CompilerParams(vmem_limit_bytes=48 * 1024 * 1024),
        cost_estimate=pl.CostEstimate(flops=4_000_000_000, bytes_accessed=6_000_000, transcendentals=0),
        name="warp_correlate",
    )(source, interp, chosen, left, turn, right, spectrum)


def correlate_in_halves(place, own, other, interp, chosen, spectrum, tables, beams, segments):
    left, right, turn, halves = tables
    points, lines = turn.shape[0], own.shape[0] * own.shape[1] // BLOCK
    column, *scratch = correlate_shapes(points, len(complex_rows(1, beams)))
    scratch += [((2, lines, BLOCK), F32), ((2, lines, BLOCK), F32)]
    rows = segments // 2 * beams * 2 * (points // segments)
    columns, theirs = pl.pallas_call(
        functools.partial(first_half_kernel, beams, segments),
        out_shape=(jax.ShapeDtypeStruct(*column), jax.ShapeDtypeStruct((rows + 16, BLOCK), BF16)),
        in_specs=[SMEM] + [VMEM] * 9,
        out_specs=(VMEM, VMEM),
        scratch_shapes=[pltpu.VMEM(*shape) for shape in scratch],
        compiler_params=pltpu.CompilerParams(vmem_limit_bytes=24 * 1024 * 1024),
        cost_estimate=pl.CostEstimate(flops=4_000_000_000, bytes_accessed=6_000_000, transcendentals=0),
        name="warp_correlate",
    )(place, own, other, interp, chosen, left, turn, right, spectrum, halves)
    mine = pl.pallas_call(
        functools.partial(second_half_kernel, beams, segments),
        out_shape=jax.ShapeDtypeStruct((rows, BLOCK), BF16),
        in_specs=[SMEM, VMEM, VMEM],
        out_specs=VMEM,
        compiler_params=pltpu.CompilerParams(vmem_limit_bytes=16 * 1024 * 1024),
        cost_estimate=pl.CostEstimate(flops=1_000_000_000, bytes_accessed=2_000_000, transcendentals=0),
        name="second_half",
    )(place, columns, halves)
    return theirs, mine


def finish_kernel(count, power_ref, sums_ref, out_ref, scratch_ref):
    hyp = pl.program_id(0)
    sums = sums_ref[...].astype(F32)
    place = lax.broadcasted_iota(jnp.int32, sums.shape, 1)
    picked = jnp.where((place >= 3 * hyp) & (place < 3 * hyp + 3), sums, 0.0)
    total = jnp.sum(jnp.sum(picked, axis=0), axis=0, keepdims=True)
    inverse = 1.0 / (total / count + 1e-06)
    devices, lines, _ = power_ref.shape
    for device in range(devices):
        scratch_ref[device * lines : (device + 1) * lines, :] = power_ref[device].astype(F32) * inverse
    beams = out_ref.shape[1]
    step = devices * lines // beams
    for line in range(step):
        half, block = divmod(line, step // 2)
        lane = block * PAIR + half * BLOCK
        out_ref[0, :, lane : lane + BLOCK] = scratch_ref[pl.ds(line, beams, stride=step), :].astype(BF16)


def finish(received, count, beams):
    segments, out_rows, _ = received.shape
    lines = (out_rows - 16) // HYPS
    samples = lines // beams * BLOCK
    return pl.pallas_call(
        functools.partial(finish_kernel, count),
        grid=(HYPS,),
        out_shape=jax.ShapeDtypeStruct((HYPS, segments * beams, samples), BF16),
        in_specs=[
            pl.BlockSpec((segments, lines, BLOCK), lambda g: (0, g, 0)),
            pl.BlockSpec((segments, 16, BLOCK), lambda g: (0, HYPS * lines // 16, 0)),
        ],
        out_specs=pl.BlockSpec((1, segments * beams, samples), lambda g: (g, 0, 0)),
        scratch_shapes=[pltpu.VMEM((segments * lines, BLOCK), F32)],
        cost_estimate=pl.CostEstimate(flops=1_000_000, bytes_accessed=1_200_000, transcendentals=0),
        name="scale_power",
    )(received, received)


def chip_order(chips):
    far, near = range(chips // 2, chips), [*range(1, chips // 2), 0]
    return [offset for pair in zip(far, near) for offset in pair][:-1] + [0]


def arrange_kernel(place_ref, mine_ref, sums_ref, got_ref, *out_refs):
    chip = place_ref[0] // 2
    count = len(out_refs)
    lines = mine_ref.shape[0] // count
    tails = [ref[count * lines :, :] for ref in (sums_ref, got_ref)]
    tail = tail_of([total[:, :1] for total in totals_of(tails)])
    for offset, out_ref in zip(chip_order(count), out_refs):
        rows = pl.ds(pl.multiple_of((chip ^ offset) * lines, lines), lines)
        out_ref[:lines, :] = mine_ref[rows, :]
        out_ref[lines : 2 * lines, :] = got_ref[rows, :]
        out_ref[2 * lines :, :] = tail


def arrange(place, mine, theirs, got, chips):
    lines = mine.shape[0] // chips
    shape = jax.ShapeDtypeStruct((2 * lines + 16, BLOCK), BF16)
    return pl.pallas_call(
        arrange_kernel,
        out_shape=[shape] * chips,
        in_specs=[SMEM] + [VMEM] * 3,
        out_specs=[VMEM] * chips,
        compiler_params=pltpu.CompilerParams(vmem_limit_bytes=16 * 1024 * 1024),
        cost_estimate=pl.CostEstimate(flops=1_000_000, bytes_accessed=1_200_000, transcendentals=0),
        name="arrange_chips",
    )(place, mine, theirs, got)


def join_kernel(count, place_ref, *refs):
    chunk_refs, out_ref, scratch_ref = refs[:-2], refs[-2], refs[-1]
    chip, core = place_ref[0] // 2, place_ref[0] % 2
    lines = chunk_refs[0].shape[0] - 16
    totals = totals_of([ref[lines:, :] for ref in chunk_refs])
    inverse = [1.0 / (total / count + 1e-06) for total in totals]
    run = lines // 2
    for part in range(2):
        hyp = core ^ part
        scale = jnp.where(hyp == 0, inverse[0], inverse[1])
        for offset, ref in zip(chip_order(len(chunk_refs)), chunk_refs):
            rows = pl.ds(pl.multiple_of((chip ^ offset) * run, run), run)
            scratch_ref[hyp, rows, :] = ref[part * run : (part + 1) * run, :].astype(F32) * scale
    beams = out_ref.shape[1]
    step = scratch_ref.shape[1] // beams
    for hyp in range(HYPS):
        for line in range(step):
            half, block = divmod(line, step // 2)
            lane = block * PAIR + half * BLOCK
            out_ref[hyp, :, lane : lane + BLOCK] = scratch_ref[hyp, pl.ds(line, beams, stride=step), :].astype(BF16)


def join(place, chunks, count, beams):
    lines = chunks[0].shape[0] - 16
    rows = lines // HYPS * len(chunks)
    return pl.pallas_call(
        functools.partial(join_kernel, count),
        out_shape=jax.ShapeDtypeStruct((HYPS, beams, rows // beams * BLOCK), BF16),
        in_specs=[SMEM] + [VMEM] * len(chunks),
        out_specs=VMEM,
        scratch_shapes=[pltpu.VMEM((HYPS, rows, BLOCK), F32)],
        compiler_params=pltpu.CompilerParams(vmem_limit_bytes=16 * 1024 * 1024),
        cost_estimate=pl.CostEstimate(flops=1_000_000, bytes_accessed=1_200_000, transcendentals=0),
        name="scale_power",
    )(place, *chunks)


def exchange(value, offset, segments):
    return lax.ppermute(value, "tm", [(index, index ^ offset) for index in range(segments)])


def body(signal, warp_blocks, taps, tap_weights, replica):
    segments = lax.axis_size("tm")
    beams = signal.shape[0] // segments
    samples = signal.shape[1] * segments
    count = float(BEAMS * samples)
    paired = segments == 16
    place = lax.axis_index("tm").astype(jnp.int32).reshape(1)
    tables = transform_tables(samples // PAIR, segments)
    prepared = prepare(place, replica, taps, tap_weights, warp_blocks, tables, segments, paired)
    if not paired:
        received = lax.all_to_all(spread(signal, segments), "tm", split_axis=0, concat_axis=0, tiled=True)
        sent = correlate(received.reshape(-1, BLOCK), *prepared, tables, beams, segments)
        back = lax.all_to_all(sent, "tm", split_axis=0, concat_axis=0, tiled=True)
        return finish(back, count, beams)
    groups = [list(range(core, segments, 2)) for core in range(2)]
    own = lax.all_to_all(
        signal.reshape(segments // 2, 2 * beams, -1), "tm", 0, 0, axis_index_groups=groups, tiled=True
    ).reshape(signal.shape)
    own, *prepared = lax.optimization_barrier((own, *prepared))
    other = exchange(own, 1, segments)
    theirs, mine = correlate_in_halves(place, own, other, *prepared, tables, 2 * beams, segments)
    chips = segments // 2
    chunks = arrange(place, mine, theirs, exchange(theirs, 1, segments), chips)
    arrived = [
        exchange(chunk, 2 * offset, segments) if offset else chunk for offset, chunk in zip(chip_order(chips), chunks)
    ]
    return join(place, arrived, count, signal.shape[0])


def solution(mesh):
    in_specs = (
        P("groups", "tm"),
        P("groups", None),
        P("groups", None, None),
        P("groups", None, None),
        P(),
    )
    out_specs = P("groups", None, "tm")
    return jax.shard_map(body, mesh=mesh, in_specs=in_specs, out_specs=out_specs, check_vma=False)
```

```python
import functools
import math

import jax
import jax.numpy as jnp
import numpy as np
from jax import lax
from jax.experimental import pallas as pl
from jax.experimental.pallas import tpu as pltpu
from jax.sharding import PartitionSpec as P

BEAMS = 64
BLOCK = 128
PAIR = 2 * BLOCK
TAPS = 8
REPLICA = 16384
HYPS = 2
TAIL = 8
F32 = jnp.float32
BF16 = jnp.bfloat16
VMEM = pl.BlockSpec(memory_space=pltpu.VMEM)
SMEM = pl.BlockSpec(memory_space=pltpu.SMEM)
ANY = pl.BlockSpec(memory_space=pl.ANY)


def transform_tables(points, segments):
    k, p = np.arange(points)[:, None], np.arange(points)[None, :]
    angle = 2.0 * math.pi * (k * p % points) / points
    cos, sin = np.cos(angle), np.sin(angle)
    left = np.block([[cos, sin], [-sin, cos]]).astype(np.float32)
    k, p = np.arange(PAIR)[:, None], np.arange(PAIR)[None, :]
    angle = 2.0 * math.pi * (k * p % PAIR) / PAIR
    cos, sin = np.cos(angle), np.sin(angle)
    right = np.block([[cos, -sin], [sin, cos]]).astype(np.float32)
    k, q = np.arange(points)[:, None], np.arange(PAIR)[None, :]
    angle = 2.0 * math.pi * (k * q) / (points * PAIR)
    turn = np.concatenate([np.cos(angle), -np.sin(angle)], axis=1).astype(np.float32)
    parts = []
    for table in (left, right):
        high = table.astype(jnp.bfloat16)
        low = (table - high.astype(np.float32)).astype(jnp.bfloat16)
        parts.append(np.concatenate([high, low], axis=0))
    halves = parts[0].reshape(4, segments // 2, 2, points // segments, 2 * points).transpose(2, 0, 1, 3, 4)
    halves = halves.reshape(2, 2 * points, 2 * points)
    return jnp.asarray(parts[0]), jnp.asarray(parts[1]), jnp.asarray(turn), jnp.asarray(halves)


def split(value):
    high = value.astype(BF16)
    return high, (value - high.astype(F32)).astype(BF16)


def dot(left, right):
    return jnp.dot(left, right, preferred_element_type=F32)


def spread(signal, segments):
    beams, blocks = signal.shape[0] // segments, signal.shape[1] // BLOCK
    send = signal.reshape(segments, beams, blocks, BLOCK).transpose(0, 2, 1, 3)
    return send.reshape(segments, blocks * beams, BLOCK)


def prepare_kernel(
    segments, paired, place_ref, replica_ref, taps_ref, weights_ref, sources_ref, left_ref, right_ref, turn_ref, interp_ref, chosen_ref, spectrum_ref
):
    core = place_ref[0] % 2
    blocks = chosen_ref.shape[1]
    points = blocks // 2
    window = lax.broadcasted_iota(jnp.int32, (PAIR, BLOCK), 0)
    row = lax.broadcasted_iota(jnp.int32, (blocks, blocks), 0)
    column = lax.broadcasted_iota(jnp.int32, (blocks, blocks), 1)
    order = (column == row % points * 2 + row // points).astype(F32).astype(BF16)
    held = row
    if paired:
        chips, local = segments // 2, blocks // segments
        held = row % chips * 2 * local + (row // points + core) % 2 * local + row // chips % local
    for index, hyp in enumerate([core] if paired else range(HYPS)):
        taps, weights = taps_ref[hyp], weights_ref[hyp]
        total = jnp.zeros((PAIR, BLOCK), F32)
        for tap in range(TAPS):
            total = total + jnp.where(taps[tap : tap + 1, :] == window, weights[tap : tap + 1, :], 0.0)
        if paired:
            interp_ref[...] = jnp.concatenate([total[:BLOCK], total[BLOCK:]], axis=1).astype(BF16)
        else:
            interp_ref[:, hyp * BLOCK : (hyp + 1) * BLOCK] = total.astype(BF16)
        hits = (held == sources_ref[pl.ds(hyp, 1), :]).astype(F32).astype(BF16)
        picked = lax.dot_general(order, hits, (((1,), (1,)), ((), ())), preferred_element_type=F32)
        chosen_ref[index * blocks : (index + 1) * blocks, :] = picked.astype(BF16)

    lines = replica_ref.shape[0] // 2
    high, low = split(jnp.concatenate([replica_ref[pl.ds(half, lines, stride=2), :] for half in range(2)], axis=1))
    both = dot(left_ref[:, :lines], high)
    value = both[: 2 * points] + both[2 * points :] + dot(left_ref[: 2 * points, :lines], low)
    value_re, value_im = value[:points], value[points:]
    turn_re, turn_im = turn_ref[:, :PAIR], turn_ref[:, PAIR:]
    turned = jnp.concatenate(
        [value_re * turn_re - value_im * turn_im, value_re * turn_im + value_im * turn_re], axis=1
    )
    high, low = split(turned)
    upper, lower = right_ref[: 2 * PAIR, :], right_ref[2 * PAIR :, :]
    value = (dot(high, upper) + dot(high, lower) + dot(low, upper)) * (1.0 / (points * PAIR))
    spectrum_ref[:, :PAIR] = value[:, :PAIR]
    spectrum_ref[:, PAIR:] = -value[:, PAIR:]


def prepare(place, replica, taps, tap_weights, warp_blocks, tables, segments, paired):
    blocks = warp_blocks.shape[1]
    points = blocks // 2
    taps, tap_weights = taps.transpose(0, 2, 1), tap_weights.transpose(0, 2, 1)
    operands = (replica.reshape(-1, BLOCK), taps, tap_weights, warp_blocks, *tables[:3])
    interp, count = ((BLOCK, PAIR), 1) if paired else ((PAIR, HYPS * BLOCK), HYPS)
    shapes = (interp, BF16), ((count * blocks, blocks), BF16), ((points, 2 * PAIR), F32)

    def whole(shape):
        return pl.BlockSpec(shape, lambda g: (0,) * len(shape))

    return pl.pallas_call(
        functools.partial(prepare_kernel, segments, paired),
        grid=(1,),
        out_shape=[jax.ShapeDtypeStruct(*shape) for shape in shapes],
        in_specs=[SMEM] + [whole(operand.shape) for operand in operands],
        out_specs=[VMEM] * len(shapes),
        compiler_params=pltpu.CompilerParams(vmem_limit_bytes=24 * 1024 * 1024),
        cost_estimate=pl.CostEstimate(flops=500_000_000, bytes_accessed=16_000_000, transcendentals=0),
        name="prepare_tables",
    )(place, *operands)


def split_sum(total):
    high = total.astype(BF16).astype(F32)
    middle = (total - high).astype(BF16).astype(F32)
    return high, middle, total - high - middle


def tail_of(totals):
    place = lax.broadcasted_iota(jnp.int32, (TAIL, BLOCK), 0)
    tail = jnp.zeros((TAIL, BLOCK), F32)
    for hyp, total in enumerate(totals):
        for index, piece in enumerate(split_sum(total)):
            tail = jnp.where(place == hyp * 3 + index, piece, tail)
    return tail.astype(BF16)


def totals_of(tails):
    place = lax.broadcasted_iota(jnp.int32, (TAIL, BLOCK), 0)
    total = functools.reduce(jnp.add, [tail.astype(F32) for tail in tails])
    return [
        jnp.sum(jnp.where((place >= 3 * hyp) & (place < 3 * hyp + 3), total, 0.0), axis=0, keepdims=True)
        for hyp in range(HYPS)
    ]


def complex_rows(hyps, beams):
    if beams % 2:
        return [(hyp, beam, None) for hyp in range(hyps) for beam in range(beams)]
    return [(hyp, beam, beam + 1) for hyp in range(hyps) for beam in range(0, beams, 2)]


def warp(beams, source_ref, interp_ref, chosen_ref, column_ref, next_ref, block_ref):
    lines = source_ref.shape[0]
    blocks = lines // beams
    chunk = min(512, lines)

    for start in range(0, lines, chunk):
        next_ref[start : start + chunk, :] = dot(source_ref[start : start + chunk, :], interp_ref[BLOCK:, :])
    next_ref[lines : lines + 8, :] = next_ref[0:8, :]
    for start in range(0, lines, chunk):
        value = (
            dot(source_ref[start : start + chunk, :], interp_ref[:BLOCK, :])
            + next_ref[start + beams : start + beams + chunk, :]
        )
        for hyp in range(HYPS):
            block_ref[hyp, start : start + chunk, :] = value[:, hyp * BLOCK : (hyp + 1) * BLOCK]
    for hyp in range(HYPS):
        warped = jnp.concatenate(
            [block_ref[hyp, pl.ds(beam, blocks, stride=beams), :].astype(BF16) for beam in range(beams)], axis=1
        )
        choose(hyp, HYPS, beams, chosen_ref[hyp * blocks : (hyp + 1) * blocks, :], warped, column_ref)


def choose(hyp, hyps, beams, chosen, warped, column_ref):
    gathered = dot(chosen, warped).astype(BF16)
    points = gathered.shape[0] // 2
    for index, (row_hyp, *pair) in enumerate(complex_rows(hyps, beams)):
        if row_hyp != hyp:
            continue
        for part, beam in enumerate(pair):
            for half in range(2):
                lane = index * PAIR + half * BLOCK
                target = (slice(part * points, (part + 1) * points), slice(lane, lane + BLOCK))
                if beam is None:
                    column_ref[target] = jnp.zeros((points, BLOCK), BF16)
                else:
                    column_ref[target] = gathered[
                        half * points : (half + 1) * points, beam * BLOCK : (beam + 1) * BLOCK
                    ]


def warp_paired(beams, core, own_ref, other_ref, interp_ref, chosen_ref, column_ref, next_ref, block_ref):
    lines, samples = own_ref.shape
    local = samples // BLOCK
    for part, source_ref in enumerate((own_ref, other_ref)):
        stacked = jnp.concatenate(
            [source_ref[:, block * BLOCK : (block + 1) * BLOCK] for block in range(local)], axis=0
        )
        value = dot(stacked, interp_ref[...])
        block_ref[part] = value[:, :BLOCK]
        next_ref[part] = value[:, BLOCK:]
    last = (local - 1) * lines
    for part in range(2):
        block_ref[part, :last, :] = block_ref[part, :last, :] + next_ref[part, lines:, :]
        after = next_ref[1 - part, :lines, :]
        turned = jnp.concatenate([after[beams:], after[:beams]], axis=0)
        block_ref[part, last:, :] = block_ref[part, last:, :] + jnp.where((core + part) % 2 == 0, after, turned)
    count = local * lines // beams
    warped = [
        jnp.concatenate(
            [block_ref[part, pl.ds(beam, count, stride=beams), :].astype(BF16) for beam in range(beams)], axis=1
        )
        for part in range(2)
    ]
    choose(0, 1, beams, chosen_ref[...], jnp.concatenate(warped, axis=0), column_ref)


def transform(hyps, beams, left_ref, turn_ref, right_ref, spectrum_ref, column_ref, row_ref, wide_ref):
    points = turn_ref.shape[0]
    rows = complex_rows(hyps, beams)

    def right_product():
        value = row_ref[...]
        wide_ref[...] = dot(value, right_ref[: 2 * PAIR, :]) + dot(value, right_ref[2 * PAIR :, :])

    turn_re, turn_im = turn_ref[:, :PAIR], turn_ref[:, PAIR:]
    for index in range(len(rows)):
        real, imag = left_product(left_ref[...], column_ref, index)
        place = slice(index * points, (index + 1) * points)
        row_ref[place, :PAIR] = (real * turn_re - imag * turn_im).astype(BF16)
        row_ref[place, PAIR:] = (real * turn_im + imag * turn_re).astype(BF16)
    right_product()
    spectrum_re, spectrum_im = spectrum_ref[:, :PAIR], spectrum_ref[:, PAIR:]
    sums = [jnp.zeros((8, PAIR), F32) for _ in range(hyps)]
    for index, (hyp, _, _) in enumerate(rows):
        place = slice(index * points, (index + 1) * points)
        real, imag = wide_ref[place, :PAIR], wide_ref[place, PAIR:]
        new_re = real * spectrum_re - imag * spectrum_im
        new_im = real * spectrum_im + imag * spectrum_re
        square = new_re * new_re + new_im * new_im
        sums[hyp] = sums[hyp] + jnp.sum(square.reshape(points // 8, 8, PAIR), axis=0)
        row_ref[place, PAIR:] = new_re.astype(BF16)
        row_ref[place, :PAIR] = new_im.astype(BF16)
    right_product()
    for index in range(len(rows)):
        place = slice(index * points, (index + 1) * points)
        lanes = slice(index * PAIR, (index + 1) * PAIR)
        imag, real = wide_ref[place, :PAIR], wide_ref[place, PAIR:]
        column_ref[points:, lanes] = (real * turn_re + imag * turn_im).astype(BF16)
        column_ref[:points, lanes] = (imag * turn_re - real * turn_im).astype(BF16)
    return [
        jnp.sum(jnp.sum(value, axis=1, keepdims=True), axis=0, keepdims=True) * (points * PAIR) for value in sums
    ]


def left_product(matrix, column_ref, index):
    both = dot(matrix, column_ref[:, index * PAIR : (index + 1) * PAIR])
    value = both[: both.shape[0] // 2] + both[both.shape[0] // 2 :]
    return value[: value.shape[0] // 2], value[value.shape[0] // 2 :]


def store_powers(matrix, column_ref, hyps, beams, segments, target):
    for index, (hyp, real_beam, imag_beam) in enumerate(complex_rows(hyps, beams)):
        imag, real = left_product(matrix, column_ref, index)
        for beam, value in ((real_beam, real), (imag_beam, imag)):
            if beam is None:
                continue
            number = hyp * beams + beam
            power = value * value
            share = power.shape[0] // segments
            for segment in range(segments):
                piece = power[segment * share : (segment + 1) * share, :]
                piece = jnp.concatenate([piece[:, :BLOCK], piece[:, BLOCK:]], axis=0)
                target(segment)[number * 2 * share : (number + 1) * 2 * share, :] = piece.astype(BF16)


def correlate_kernel(beams, segments, source_ref, interp_ref, chosen_ref, left_ref, turn_ref, right_ref, spectrum_ref, *refs):
    out_ref, column_ref, row_ref, wide_ref, next_ref, block_ref = refs
    warp(beams, source_ref, interp_ref, chosen_ref, column_ref, next_ref, block_ref)
    totals = transform(HYPS, beams, left_ref, turn_ref, right_ref, spectrum_ref, column_ref, row_ref, wide_ref)
    store_powers(left_ref[...], column_ref, HYPS, beams, segments, lambda segment: out_ref.at[segment])
    tail = tail_of(totals)
    for segment in range(segments):
        out_ref[segment, out_ref.shape[1] - TAIL :, :] = tail


def first_half_kernel(
    beams, segments, place_ref, own_ref, other_ref, interp_ref, chosen_ref, left_ref, turn_ref, right_ref, spectrum_ref, halves_ref, *refs
):
    column_ref, theirs_ref, row_ref, wide_ref, next_ref, block_ref = refs
    core = place_ref[0] % 2
    warp_paired(beams, core, own_ref, other_ref, interp_ref, chosen_ref, column_ref, next_ref, block_ref)
    (total,) = transform(1, beams, left_ref, turn_ref, right_ref, spectrum_ref, column_ref, row_ref, wide_ref)
    chips = segments // 2
    lines = (theirs_ref.shape[0] - TAIL) // chips
    store_powers(
        halves_ref[1 - core], column_ref, 1, beams, chips, lambda chip: theirs_ref.at[chip * lines : (chip + 1) * lines]
    )
    theirs_ref[chips * lines :, :] = tail_of([jnp.where(core == hyp, total, 0.0) for hyp in range(HYPS)])


def second_half_kernel(beams, segments, place_ref, column_ref, halves_ref, mine_ref):
    chips = segments // 2
    lines = mine_ref.shape[0] // chips
    store_powers(
        halves_ref[place_ref[0] % 2],
        column_ref,
        1,
        beams,
        chips,
        lambda chip: mine_ref.at[chip * lines : (chip + 1) * lines],
    )


def correlate_shapes(points, count):
    return (
        ((2 * points, count * PAIR), BF16),
        ((count * points, 2 * PAIR), BF16),
        ((count * points, 2 * PAIR), F32),
    )


def correlate(source, interp, chosen, spectrum, tables, beams, segments):
    left, right, turn, _ = tables
    points, lines = turn.shape[0], source.shape[0]
    scratch = correlate_shapes(points, len(complex_rows(HYPS, beams)))
    scratch += (((lines + 8, PAIR), F32), ((HYPS, lines, BLOCK), F32))
    return pl.pallas_call(
        functools.partial(correlate_kernel, beams, segments),
        out_shape=jax.ShapeDtypeStruct((segments, HYPS * beams * 2 * (points // segments) + TAIL, BLOCK), BF16),
        in_specs=[VMEM] * 7,
        out_specs=VMEM,
        scratch_shapes=[pltpu.VMEM(*shape) for shape in scratch],
        compiler_params=pltpu.CompilerParams(vmem_limit_bytes=48 * 1024 * 1024),
        cost_estimate=pl.CostEstimate(flops=4_000_000_000, bytes_accessed=6_000_000, transcendentals=0),
        name="warp_correlate",
    )(source, interp, chosen, left, turn, right, spectrum)


def correlate_in_halves(place, own, other, interp, chosen, spectrum, tables, beams, segments):
    left, right, turn, halves = tables
    points, lines = turn.shape[0], own.shape[0] * own.shape[1] // BLOCK
    column, *scratch = correlate_shapes(points, len(complex_rows(1, beams)))
    scratch += [((2, lines, BLOCK), F32), ((2, lines, BLOCK), F32)]
    rows = segments // 2 * beams * 2 * (points // segments)
    columns, theirs = pl.pallas_call(
        functools.partial(first_half_kernel, beams, segments),
        out_shape=(jax.ShapeDtypeStruct(*column), jax.ShapeDtypeStruct((rows + TAIL, BLOCK), BF16)),
        in_specs=[SMEM] + [VMEM] * 9,
        out_specs=(VMEM, VMEM),
        scratch_shapes=[pltpu.VMEM(*shape) for shape in scratch],
        compiler_params=pltpu.CompilerParams(vmem_limit_bytes=24 * 1024 * 1024),
        cost_estimate=pl.CostEstimate(flops=4_000_000_000, bytes_accessed=6_000_000, transcendentals=0),
        name="warp_correlate",
    )(place, own, other, interp, chosen, left, turn, right, spectrum, halves)
    mine = pl.pallas_call(
        functools.partial(second_half_kernel, beams, segments),
        out_shape=jax.ShapeDtypeStruct((rows, BLOCK), BF16),
        in_specs=[SMEM, VMEM, VMEM],
        out_specs=VMEM,
        compiler_params=pltpu.CompilerParams(vmem_limit_bytes=16 * 1024 * 1024),
        cost_estimate=pl.CostEstimate(flops=1_000_000_000, bytes_accessed=2_000_000, transcendentals=0),
        name="second_half",
    )(place, columns, halves)
    return theirs, mine


def finish_kernel(count, power_ref, sums_ref, out_ref, scratch_ref):
    hyp = pl.program_id(0)
    sums = sums_ref[...].astype(F32)
    place = lax.broadcasted_iota(jnp.int32, sums.shape, 1)
    picked = jnp.where((place >= 3 * hyp) & (place < 3 * hyp + 3), sums, 0.0)
    total = jnp.sum(jnp.sum(picked, axis=0), axis=0, keepdims=True)
    inverse = 1.0 / (total / count + 1e-06)
    devices, lines, _ = power_ref.shape
    for device in range(devices):
        scratch_ref[device * lines : (device + 1) * lines, :] = power_ref[device].astype(F32) * inverse
    beams = out_ref.shape[1]
    step = devices * lines // beams
    for line in range(step):
        half, block = divmod(line, step // 2)
        lane = block * PAIR + half * BLOCK
        out_ref[0, :, lane : lane + BLOCK] = scratch_ref[pl.ds(line, beams, stride=step), :].astype(BF16)


def finish(received, count, beams):
    segments, out_rows, _ = received.shape
    lines = (out_rows - TAIL) // HYPS
    samples = lines // beams * BLOCK
    return pl.pallas_call(
        functools.partial(finish_kernel, count),
        grid=(HYPS,),
        out_shape=jax.ShapeDtypeStruct((HYPS, segments * beams, samples), BF16),
        in_specs=[
            pl.BlockSpec((segments, lines, BLOCK), lambda g: (0, g, 0)),
            pl.BlockSpec((segments, TAIL, BLOCK), lambda g: (0, HYPS * lines // TAIL, 0)),
        ],
        out_specs=pl.BlockSpec((1, segments * beams, samples), lambda g: (g, 0, 0)),
        scratch_shapes=[pltpu.VMEM((segments * lines, BLOCK), F32)],
        cost_estimate=pl.CostEstimate(flops=1_000_000, bytes_accessed=1_200_000, transcendentals=0),
        name="scale_power",
    )(received, received)


CHIP_ORDER = (4, 2, 5, 1, 7, 3, 6, 0)


def arrange_kernel(place_ref, mine_ref, sums_ref, got_ref, *out_refs):
    chip = place_ref[0] // 2
    count = len(out_refs)
    lines = mine_ref.shape[0] // count
    tails = [ref[count * lines :, :] for ref in (sums_ref, got_ref)]
    tail = tail_of([total[:, :1] for total in totals_of(tails)])
    for offset, out_ref in zip(CHIP_ORDER, out_refs):
        rows = pl.ds(pl.multiple_of((chip ^ offset) * lines, lines), lines)
        out_ref[:lines, :] = mine_ref[rows, :]
        out_ref[lines : 2 * lines, :] = got_ref[rows, :]
        out_ref[2 * lines :, :] = tail


def arrange(place, mine, theirs, got, chips):
    lines = mine.shape[0] // chips
    shape = jax.ShapeDtypeStruct((2 * lines + TAIL, BLOCK), BF16)
    return pl.pallas_call(
        arrange_kernel,
        out_shape=[shape] * chips,
        in_specs=[SMEM] + [VMEM] * 3,
        out_specs=[VMEM] * chips,
        compiler_params=pltpu.CompilerParams(vmem_limit_bytes=16 * 1024 * 1024),
        cost_estimate=pl.CostEstimate(flops=1_000_000, bytes_accessed=1_200_000, transcendentals=0),
        name="arrange_chips",
    )(place, mine, theirs, got)


def join_kernel(count, place_ref, *refs):
    chunk_refs, out_ref, scratch_ref, held_ref, sems = refs[:-4], *refs[-4:]
    chip, core = place_ref[0] // 2, place_ref[0] % 2
    lines = chunk_refs[0].shape[0] - TAIL
    totals = totals_of([ref[lines:, :] for ref in chunk_refs])
    inverse = [1.0 / (total / count + 1e-06) for total in totals]
    run = lines // 2
    for part in range(2):
        hyp = core ^ part
        scale = jnp.where(hyp == 0, inverse[0], inverse[1])
        for offset, ref in zip(CHIP_ORDER, chunk_refs):
            rows = pl.ds(pl.multiple_of((chip ^ offset) * run, run), run)
            scratch_ref[hyp, rows, :] = ref[part * run : (part + 1) * run, :].astype(F32) * scale
    beams = out_ref.shape[1]
    step = scratch_ref.shape[1] // beams
    copies = []
    for hyp in range(HYPS):
        for line in range(step):
            half, block = divmod(line, step // 2)
            lane = block * PAIR + half * BLOCK
            held_ref[hyp, :, lane : lane + BLOCK] = scratch_ref[hyp, pl.ds(line, beams, stride=step), :].astype(BF16)
        copies.append(pltpu.make_async_copy(held_ref.at[hyp], out_ref.at[hyp], sems.at[hyp]))
        copies[-1].start()
    for copy in copies:
        copy.wait()


def join(place, chunks, count, beams):
    lines = chunks[0].shape[0] - TAIL
    rows = lines // HYPS * len(chunks)
    return pl.pallas_call(
        functools.partial(join_kernel, count),
        out_shape=jax.ShapeDtypeStruct((HYPS, beams, rows // beams * BLOCK), BF16),
        in_specs=[SMEM] + [VMEM] * len(chunks),
        out_specs=ANY,
        scratch_shapes=[
            pltpu.VMEM((HYPS, rows, BLOCK), F32),
            pltpu.VMEM((HYPS, beams, rows // beams * BLOCK), BF16),
            pltpu.SemaphoreType.DMA((HYPS,)),
        ],
        compiler_params=pltpu.CompilerParams(vmem_limit_bytes=16 * 1024 * 1024),
        cost_estimate=pl.CostEstimate(flops=1_000_000, bytes_accessed=1_200_000, transcendentals=0),
        name="scale_power",
    )(place, *chunks)


def exchange(value, offset, segments):
    return lax.ppermute(value, "tm", [(index, index ^ offset) for index in range(segments)])


def body(signal, warp_blocks, taps, tap_weights, replica):
    segments = lax.axis_size("tm")
    beams = signal.shape[0] // segments
    samples = signal.shape[1] * segments
    count = float(BEAMS * samples)
    paired = segments == 16
    place = lax.axis_index("tm").astype(jnp.int32).reshape(1)
    tables = transform_tables(samples // PAIR, segments)
    prepared = prepare(place, replica, taps, tap_weights, warp_blocks, tables, segments, paired)
    if not paired:
        received = lax.all_to_all(spread(signal, segments), "tm", split_axis=0, concat_axis=0, tiled=True)
        sent = correlate(received.reshape(-1, BLOCK), *prepared, tables, beams, segments)
        back = lax.all_to_all(sent, "tm", split_axis=0, concat_axis=0, tiled=True)
        return finish(back, count, beams)
    groups = [list(range(core, segments, 2)) for core in range(2)]
    own = lax.all_to_all(
        signal.reshape(segments // 2, 2 * beams, -1), "tm", 0, 0, axis_index_groups=groups, tiled=True
    ).reshape(signal.shape)
    own, *prepared = lax.optimization_barrier((own, *prepared))
    other = exchange(own, 1, segments)
    theirs, mine = correlate_in_halves(place, own, other, *prepared, tables, 2 * beams, segments)
    chips = segments // 2
    chunks = arrange(place, mine, theirs, exchange(theirs, 1, segments), chips)
    arrived = [
        exchange(chunk, 2 * offset, segments) if offset else chunk for offset, chunk in zip(CHIP_ORDER, chunks)
    ]
    return join(place, arrived, count, signal.shape[0])


def solution(mesh):
    in_specs = (
        P("groups", "tm"),
        P("groups", None),
        P("groups", None, None),
        P("groups", None, None),
        P(),
    )
    out_specs = P("groups", None, "tm")
    return jax.shard_map(body, mesh=mesh, in_specs=in_specs, out_specs=out_specs, check_vma=False)
```
